512 devices in a mesh: dp: 64 (over y, z), tm: 8 (over x, core).
Axes of the slice: x: 4, y: 8, z: 8, core: 2. Of those that a mesh axis runs over, the one named last changes fastest.
Arguments:
- latents: bfloat16 [16384, 48, 1024], P('dp', 'tm'), may hold values from -6 to 6
- lengths: int32 [16384], P('dp'), may hold values from 1 to 48, as said below
- plan: int32 [16384], P('dp'), may hold values from 0 to 255, as said below
- w_in: bfloat16 [1024, 1024], P(None, 'dp'), may hold values from -0.1875 to 0.1875
- w_down: bfloat16 [1024, 64], replicated, may hold values from -0.1875 to 0.1875
- w_up: bfloat16 [64, 1024], replicated, may hold values from -0.75 to 0.75
- w_out: bfloat16 [1024, 1024], P(None, 'dp'), may hold values from -0.1875 to 0.1875
- rate: float32 [1024], replicated, may hold values from 0.004 to 1.5
- gain: float32 [1024], replicated, may hold values from 0.5 to 1.5
- w_bits: bfloat16 [1024, 18], replicated, may hold values from -0.1875 to 0.1875
Outputs:
- codes: bfloat16 [18, 48, 16384], P(None, 'tm', 'dp')
- penalty: float32 [], replicated
The draws below stay inside these ranges and needn't reach their ends.
Inputs may be any that keep to these rules, and one draw needn't show every extreme that they name: `plan`: each aligned block of 256 entries is a permutation of 0 to 255. The rows of each aligned block of 256 rows share a cap on their lengths that rises with the block's index from about a third of 48 to 48; the first row of each block has exactly its cap.
All inputs are finite; a program needn't handle non-finite values.
Results may differ from the reference program's by a relative error of at most 0.0056.
Values may be sent and summed in bfloat16 or wider, within the bound.
A program may use at most 128 MiB of HBM per device.

```python
import math
import jax
import jax.numpy as jnp
from jax import lax

D = 1024
DT = 64
BITS = 18
R_DEV = 256
ROWS = 16384
FRAMES = 48
GROUP = 4


def shuffle_block(subkey):
    return jax.random.permutation(subkey, R_DEV)


def draw_plan(key, part):
    key = jax.random.fold_in(key, 5)
    subkeys = jax.random.split(key, ROWS // R_DEV)
    return jax.vmap(shuffle_block)(subkeys).reshape(ROWS).astype(jnp.int32)


def draw_lengths(key, part):
    key = jax.random.fold_in(key, 7)
    blocks = ROWS // R_DEV
    row_ids = jnp.arange(ROWS, dtype=jnp.int32)
    block_ids = row_ids // R_DEV
    limits = jnp.maximum(1, FRAMES * (blocks + 2 * block_ids) // (3 * blocks - 2))
    limits = jnp.minimum(limits, FRAMES)
    raw_bits = jax.random.randint(key, (ROWS,), 0, 1 << 20, dtype=jnp.int32)
    drawn = 1 + raw_bits % limits
    return jnp.where(row_ids % R_DEV == 0, limits, drawn).astype(jnp.int32)


def draw_latents(key, part):
    key = jax.random.fold_in(key, 11)
    base_key, direction_key, sign_key = jax.random.split(key, 3)
    blocks = ROWS // R_DEV
    direction = jax.random.normal(direction_key, (D,), jnp.float32)
    picks = jax.random.randint(sign_key, (blocks,), 0, 2, dtype=jnp.int32)
    block_ids = jnp.arange(blocks, dtype=jnp.int32)
    picks = jnp.where(block_ids == 0, 1 - picks[1], picks).astype(jnp.float32)
    base = jax.random.normal(base_key, (ROWS, FRAMES, D), jnp.float32)
    offset = 1.2 * picks
    offset_rows = jnp.repeat(offset, R_DEV)
    values = base + offset_rows[:, None, None] * direction[None, None, :]
    return jnp.clip(values, -6.0, 6.0).astype(jnp.bfloat16)


def levels(rng, extent, shards, low, largest):
    factor_of = 1.0
    for dim, blocks in shards:
        heights = jax.random.uniform(jax.random.fold_in(jax.random.fold_in(rng, 6), dim), (blocks,), jnp.float32, low / len(shards), largest / len(shards))
        factor_of = factor_of * jnp.repeat(jnp.exp(heights), extent[dim] // blocks).reshape((-1,) + (1,) * (len(extent) - 1 - dim))
    return factor_of


def scatter_about(key, extent, width, most, cuts=(), kind=jnp.bfloat16):
    entries = width * jax.random.normal(key, extent, jnp.float32)
    if cuts:
        entries = entries * levels(key, extent, cuts, -0.22, 0.18)
    return jnp.clip(entries, -most, most).astype(kind)


def setup_inputs(seed: int = 0) -> dict:
    keys = jax.random.split(jax.random.key(seed), 11)
    return {
        "latents": draw_latents(jax.random.fold_in(keys[10], 71), 0),
        "lengths": draw_lengths(jax.random.fold_in(keys[10], 71), 0),
        "plan": draw_plan(jax.random.fold_in(keys[10], 71), 0),
        "w_in": scatter_about(keys[3], (D, D), D ** -0.5, 0.1875, ((1, 64),)),
        "w_down": scatter_about(keys[4], (D, DT), D ** -0.5, 0.1875),
        "w_up": scatter_about(keys[5], (DT, D), DT ** -0.5, 0.75),
        "w_out": scatter_about(keys[6], (D, D), D ** -0.5, 0.1875, ((1, 64),)),
        "rate": jnp.clip(jnp.exp(jax.random.uniform(keys[7], (D,), jnp.float32, math.log(0.004), math.log(1.5))), 0.004, 1.5),
        "gain": jnp.clip(1.0 + 0.1 * jax.random.normal(keys[8], (D,), jnp.float32), 0.5, 1.5),
        "w_bits": scatter_about(keys[9], (D, BITS), D ** -0.5, 0.1875),
    }


def bit_entropy(logit_values):
    scaled = 4.0 * logit_values
    chance = jax.nn.sigmoid(scaled)
    return chance * jax.nn.softplus(-scaled) + (1.0 - chance) * jax.nn.softplus(scaled)

def reference(latents, lengths, plan, w_in, w_down, w_up, w_out, rate, gain, w_bits):

    def one_block(inputs):
        working, span = inputs
        flattened = working.reshape(R_DEV * FRAMES, D)
        drive = jnp.dot(flattened, w_in, preferred_element_type=jnp.float32).reshape(R_DEV, FRAMES, D)
        narrow = jnp.dot(flattened, w_down, preferred_element_type=jnp.float32).astype(jnp.bfloat16)
        stride = jax.nn.softplus(jnp.dot(narrow, w_up, preferred_element_type=jnp.float32))
        decay = jnp.exp(-rate[None, :] * stride).reshape(R_DEV, FRAMES, D)
        valid = (jnp.arange(FRAMES, dtype=jnp.int32)[None, :] < span[:, None]).astype(jnp.float32)

        def advance(running, frame_inputs):
            fading, pushed, masked = frame_inputs
            running = fading * running + masked[:, None] * pushed
            return (running, running)
        _, states = lax.scan(advance, jnp.zeros((R_DEV, D), jnp.float32), (jnp.swapaxes(decay, 0, 1), jnp.swapaxes(drive, 0, 1), jnp.swapaxes(valid, 0, 1)))
        rounded = jnp.swapaxes(states, 0, 1).astype(jnp.bfloat16).reshape(R_DEV * FRAMES, D)
        mixed = flattened.astype(jnp.float32) + jnp.dot(rounded, w_out, preferred_element_type=jnp.float32)
        scaling = lax.rsqrt(lax.optimization_barrier(jnp.mean(mixed * mixed, axis=1, keepdims=True)) + 1e-06)
        normed = (mixed * scaling * gain[None, :]).astype(jnp.bfloat16)
        logit_values = jnp.dot(normed, w_bits, preferred_element_type=jnp.float32)
        weight_mask = valid.reshape(R_DEV * FRAMES, 1)
        chance = jax.nn.sigmoid(4.0 * logit_values)
        totals = (lax.optimization_barrier(jnp.sum(chance * weight_mask, axis=0)), jnp.sum(bit_entropy(logit_values) * weight_mask), jnp.sum(jnp.square(jnp.abs(logit_values) - 1.0) * weight_mask), jnp.sum(valid))
        return (logit_values.astype(jnp.bfloat16).reshape(R_DEV, FRAMES, BITS), totals)
    blocks = ROWS // R_DEV
    coded, totals = lax.map(one_block, (latents.reshape(blocks, R_DEV, FRAMES, D), lengths.reshape(blocks, R_DEV)))
    chance_sum = lax.optimization_barrier(jnp.sum(totals[0], axis=0))
    entropy_sum = jnp.sum(totals[1])
    commit_sum = jnp.sum(totals[2])
    count = jnp.sum(totals[3])
    marginal = chance_sum / count
    batch_entropy = jnp.sum(-marginal * jnp.log(marginal) - (1.0 - marginal) * jnp.log(1.0 - marginal))
    slots = float(ROWS * FRAMES)
    penalty = entropy_sum / slots - batch_entropy + 0.25 * commit_sum / slots
    coded = coded.reshape(ROWS, FRAMES, BITS)
    index = jnp.arange(ROWS, dtype=jnp.int32)
    target_dev = index // R_DEV
    within = index % R_DEV
    source_dev = within // GROUP
    position = within % GROUP
    source_row = source_dev * R_DEV + plan[source_dev * R_DEV + target_dev * GROUP + position]
    placed = jnp.transpose(coded[source_row], (2, 1, 0))
    return (placed, penalty)
```

```python
import functools
import math

import jax
import jax.numpy as jnp
from jax import lax
from jax.experimental import pallas as pl
from jax.experimental.pallas import tpu as pltpu
from jax.sharding import PartitionSpec as P

MESH = pl.DeviceIdType.MESH
GROUP = 4
LANES = 128
CHUNKS = 4
LOG2E = math.log2(math.e)


def nt(a, b):
    return lax.dot_general(a, b, (((1,), (1,)), ((), ())), preferred_element_type=jnp.float32)


def nn(a, b):
    return jnp.dot(a, b, preferred_element_type=jnp.float32)


def kernel(
    dp_count, tm_count, x_hbm, lengths_ref, plan_ref, win_ref, wdown_ref, wup_ref, wout_ref, rate_ref,
    gain_ref, wbits_ref, codes_ref, penalty_ref,
    x_ref, wt, narrow, dec, drv, reach, local, ent, leave, states, mixed, wb, onehot, pick, len_b,
    logits, sendbuf, recvbuf, tmbuf,
    x_sem, p1_send, p1_recv, ring_send, ring_recv, sib_send, sib_recv, chain_send, chain_recv,
    a2a_send, a2a_recv, tm_send, tm_recv,
):
    frames, rows, width = x_ref.shape
    n = math.isqrt(dp_count)
    half = width // 2
    block = width // dp_count
    part = rows // CHUNKS
    tile = min(256, width)
    tiles = width // tile
    bits = wbits_ref.shape[0]
    packed = bits * frames
    me = lax.axis_index("dp")
    tm = lax.axis_index("tm")
    y, z = me // n, me % n
    core = tm % 2
    major = y * (1 - core) + z * core
    minor = z * (1 - core) + y * core

    def dp_of(major_id, minor_id):
        return (major_id * n + minor_id) * (1 - core) + (minor_id * n + major_id) * core

    def on_core(make):
        pl.when(core == 0)(lambda: make(0))
        pl.when(core == 1)(lambda: make(1))

    right = dp_of((major + 1) % n, minor)
    left = dp_of((major + n - 1) % n, minor)
    sibling = tm + 1 - 2 * core

    x_copy = pltpu.make_async_copy(x_hbm, x_ref, x_sem)
    x_copy.start()

    barrier = pltpu.get_barrier_semaphore()
    for step in range(1, n):
        peer = dp_of(major, (minor + step) % n)
        pl.semaphore_signal(barrier, inc=1, device_id=(peer, tm), device_id_type=MESH)
    for peer in (left, right):
        pl.semaphore_signal(barrier, inc=1, device_id=(peer, tm), device_id_type=MESH)
    for step in range(1, tm_count):
        pl.semaphore_signal(
            barrier, inc=1, device_id=(me, (tm + step) % tm_count), device_id_type=MESH
        )

    for w, ref in enumerate((win_ref, wout_ref)):
        @pl.when(core == 0)
        def _():
            wt[w, 0, y, z] = ref[:, :half]

        @pl.when(core == 1)
        def _():
            wt[w, 1, y, z] = ref[:, half:]

    pl.semaphore_wait(barrier, (n - 1) + 2 + (tm_count - 1))

    def group(w, c, major_id, low=0, count=n):
        if c == 0:
            return wt.at[w, 0, major_id, pl.ds(low, count)]
        return wt.at[w, 1, pl.ds(low, count), major_id]

    for w in range(2):
        for step in range(1, n):
            pltpu.make_async_remote_copy(
                src_ref=wt.at[w, core, y, z], dst_ref=wt.at[w, core, y, z],
                send_sem=p1_send.at[w], recv_sem=p1_recv.at[w],
                device_id=(dp_of(major, (minor + step) % n), tm), device_id_type=MESH,
            ).start()

    def remote(ref, send, recv, device):
        return pltpu.make_async_remote_copy(
            src_ref=ref, dst_ref=ref, send_sem=send, recv_sem=recv,
            device_id=device, device_id_type=MESH,
        )

    def to_sibling(w, c, major_id, low=0, count=n):
        remote(
            group(w, c, major_id, low, count), sib_send.at[w], sib_recv.at[w], (me, sibling)
        ).start()

    last = n // 2

    def pieces(w, c, step, ahead):
        back = (major + n - (step - 1) - ahead) % n
        forth = (major + (step - 1) + ahead) % n
        if step < last:
            return group(w, c, back), group(w, c, forth)
        return group(w, c, back, 0, n // 2), group(w, c, forth, n // 2, n // 2)

    def ring_start(w, step):
        def make(c):
            rightward, leftward = pieces(w, c, step, 0)
            remote(
                rightward, ring_send.at[w, 0, step - 1], ring_recv.at[w, 0, step - 1], (right, tm)
            ).start()
            remote(
                leftward, ring_send.at[w, 1, step - 1], ring_recv.at[w, 1, step - 1], (left, tm)
            ).start()
        on_core(make)

    def ring_arrive(w, step):
        def make(c):
            rightward, leftward = pieces(w, c, step, 1)
            remote(
                rightward, ring_send.at[w, 0, step - 1], ring_recv.at[w, 0, step - 1], (right, tm)
            ).wait_recv()
            remote(
                leftward, ring_send.at[w, 1, step - 1], ring_recv.at[w, 1, step - 1], (left, tm)
            ).wait_recv()
            for piece in (rightward, leftward):
                remote(piece, sib_send.at[w], sib_recv.at[w], (me, sibling)).start()
        on_core(make)

    def ring_sent(w, step):
        def make(c):
            rightward, leftward = pieces(w, c, step, 0)
            remote(
                rightward, ring_send.at[w, 0, step - 1], ring_recv.at[w, 0, step - 1], (right, tm)
            ).wait_send()
            remote(
                leftward, ring_send.at[w, 1, step - 1], ring_recv.at[w, 1, step - 1], (left, tm)
            ).wait_send()
        on_core(make)

    def first_arrive(w):
        def make(c):
            remote(
                group(w, c, major, 0, n - 1), p1_send.at[w], p1_recv.at[w], (right, tm)
            ).wait_recv()
            to_sibling(w, c, major)
        on_core(make)

    def small_things():
        first = tm * frames
        lengths = jnp.broadcast_to(lengths_ref[...].astype(jnp.float32), (LANES, rows))
        len_b[...] = lengths.T - first.astype(jnp.float32)
        spread = dp_count * 8
        slot = lax.broadcasted_iota(jnp.int32, (rows, spread), 1)
        source = lax.broadcasted_iota(jnp.int32, (rows, spread), 0)
        kept = slot % 8 < GROUP
        expand = jnp.where(kept & ((slot // 8) * GROUP + slot % 8 == source), 1.0, 0.0)
        expand = expand.astype(jnp.bfloat16)
        pick[...] = expand.T
        plan_rows = jnp.broadcast_to(plan_ref[...].astype(jnp.float32), (8, rows))
        wanted = nn(plan_rows.astype(jnp.bfloat16), expand)[0:1]
        chosen = jnp.where(kept & (wanted == source.astype(jnp.float32)), 1.0, 0.0)
        onehot[...] = chosen.T.astype(jnp.bfloat16)

    def spread_bits():
        place = lax.broadcasted_iota(jnp.int32, (LANES, bits), 0)
        bit = lax.broadcasted_iota(jnp.int32, (LANES, bits), 1)
        for t in range(frames):
            chooser = jnp.where(place == bit * frames + t, 1.0, 0.0).astype(jnp.bfloat16)
            wb[t] = nn(chooser, wbits_ref[...]).astype(jnp.bfloat16)

    def narrowing():
        x_copy.wait()
        for t in range(frames):
            narrow[t] = nt(x_ref[t], wdown_ref[...]).astype(jnp.bfloat16)

    def decays(t):
        for i in range(tiles):
            cols = slice(i * tile, (i + 1) * tile)
            u = nn(narrow[t], wup_ref[:, cols]) * LOG2E
            soft = jnp.maximum(u, 0.0) + jnp.log2(1.0 + jnp.exp2(-jnp.abs(u)))
            d = jnp.exp2(-rate_ref[:, cols] * soft)
            dec[t, :, cols] = d
            reach[:, cols] = d if t == 0 else reach[:, cols] * d

    def late(step):
        if step < frames:
            decays(step)

    narrowing()
    first_arrive(0)
    ring_start(0, 1)
    first_arrive(1)
    ring_start(1, 1)
    done = 0
    for step in range(1, last + 1):
        late(done)
        done += 1
        ring_arrive(0, step)
        if step < last:
            ring_start(0, step + 1)
        ring_arrive(1, step)
        if step < last:
            ring_start(1, step + 1)
    small_things()
    spread_bits()
    while done < frames:
        late(done)
        done += 1

    def sibling_arrived(w):
        theirs = wt.at[w, 1 - core]
        remote(theirs, sib_send.at[w], sib_recv.at[w], (me, sibling)).wait_recv()

    def weight_rows(w, i):
        per = n // tiles
        both = [wt[w, c, i * per:(i + 1) * per].reshape(tile, half) for c in range(2)]
        return jnp.concatenate(both, axis=1)

    @pl.when(tm == 0)
    def _():
        ent[...] = jnp.zeros_like(ent)

    def valid_of(k, t):
        rs = slice(k * part, (k + 1) * part)
        return jnp.where(len_b[rs, :] > float(t), 1.0, 0.0)

    def drives(k):
        rs = slice(k * part, (k + 1) * part)
        left_side = x_ref[:, rs, :].reshape(frames * part, width)
        for i in range(tiles):
            cols = slice(i * tile, (i + 1) * tile)
            pushed = nt(left_side, weight_rows(0, i)).reshape(frames, part, tile)
            running = None
            for t in range(frames):
                mask = jnp.concatenate([valid_of(k, t)] * max(1, tile // LANES), axis=1)[:, :tile]
                now = pushed[t] * mask
                drv[t, rs, cols] = now
                running = now if t == 0 else dec[t, rs, cols] * running + now
            local[rs, cols] = running

    def pass_on(k):
        rs = slice(k * part, (k + 1) * part)

        @pl.when(tm > 0)
        def _():
            remote(ent.at[k], chain_send.at[k], chain_recv.at[k], (me, tm)).wait_recv()

        @pl.when(tm < tm_count - 1)
        def _():
            out = reach[rs, :] * ent[k].astype(jnp.float32) + local[rs, :]
            leave[k] = out.astype(jnp.bfloat16)
            pltpu.make_async_remote_copy(
                src_ref=leave.at[k], dst_ref=ent.at[k],
                send_sem=chain_send.at[k], recv_sem=chain_recv.at[k],
                device_id=(me, (tm + 1) % tm_count), device_id_type=MESH,
            ).start()

    def outputs(k):
        rs = slice(k * part, (k + 1) * part)
        for i in range(tiles):
            cols = slice(i * tile, (i + 1) * tile)
            s = ent[k, :, cols].astype(jnp.float32)
            for t in range(frames):
                s = dec[t, rs, cols] * s + drv[t, rs, cols]
                states[t, :, cols] = s.astype(jnp.bfloat16)
        left_side = states[...].reshape(frames * part, width)
        square = None
        for i in range(tiles):
            cols = slice(i * tile, (i + 1) * tile)
            x = x_ref[:, rs, cols].reshape(frames * part, tile).astype(jnp.float32)
            m = x + nt(left_side, weight_rows(1, i))
            mixed[:, cols] = m
            square = m * m if i == 0 else square + m * m
        scaling = lax.rsqrt(jnp.sum(square, axis=1, keepdims=True) * (1.0 / width) + 1e-06)
        total = None
        for t in range(frames):
            ts = slice(t * part, (t + 1) * part)
            normed = (mixed[ts, :] * scaling[ts, :] * gain_ref[...]).astype(jnp.bfloat16)
            term = nt(normed, wb[t])
            total = term if t == 0 else total + term
        logits[rs, :] = total

    sibling_arrived(0)
    drives(0)
    pass_on_order = []
    for k in range(CHUNKS):
        if k + 1 < CHUNKS:
            drives(k + 1)
        pass_on(k)
        if k == 0:
            sibling_arrived(1)
        outputs(k)

    values = logits[...]
    lane = lax.broadcasted_iota(jnp.int32, (rows, LANES), 1)
    frame = (lane % frames).astype(jnp.float32)
    weight = jnp.where((len_b[...] > frame) & (lane < packed), 1.0, 0.0)
    scaled = 4.0 * values
    size = jnp.abs(scaled)
    e = jnp.exp(-size)
    inverse = 1.0 / (1.0 + e)
    chance = jnp.where(scaled >= 0.0, inverse, e * inverse)
    entropy = jnp.log(1.0 + e) + size * e * inverse
    commit = jnp.square(jnp.abs(values) - 1.0)

    def summed(value):
        return jnp.sum(value * weight, axis=0, keepdims=True)

    row8 = lax.broadcasted_iota(jnp.int32, (8, LANES), 0)
    sums = jnp.zeros((8, LANES), jnp.float32)
    for row, value in enumerate((chance, entropy, commit, jnp.ones_like(weight))):
        sums = jnp.where(row8 == GROUP + row, summed(value), sums)

    dealt = nn(onehot[...], values.astype(jnp.bfloat16))
    sendbuf[...] = dealt.reshape(dp_count, 8, LANES) + sums[None]
    recvbuf[me] = sendbuf[me]

    def deal(step, carry):
        peer = (me + step) % dp_count
        pltpu.make_async_remote_copy(
            src_ref=sendbuf.at[peer], dst_ref=recvbuf.at[me], send_sem=a2a_send, recv_sem=a2a_recv,
            device_id=(peer, tm), device_id_type=MESH,
        ).start()
        return carry

    lax.fori_loop(1, dp_count, deal, 0)
    arrived = recvbuf.at[pl.ds(0, dp_count - 1)]
    remote(arrived, a2a_send, a2a_recv, (right, tm)).wait_recv()

    tmbuf[tm] = jnp.sum(recvbuf[...], axis=0)
    for step in range(1, tm_count):
        remote(tmbuf.at[tm], tm_send, tm_recv, (me, (tm + step) % tm_count)).start()

    turned = recvbuf[...].reshape(dp_count * 8, LANES).T.astype(jnp.bfloat16)
    placed = nn(turned, pick[...])
    for b in range(bits):
        codes_ref[b] = placed[b * frames:(b + 1) * frames, :].astype(jnp.bfloat16)

    remote(
        tmbuf.at[pl.ds(0, tm_count - 1)], tm_send, tm_recv, (me, sibling)
    ).wait_recv()
    totals = tmbuf[0]
    for i in range(1, tm_count):
        totals = totals + tmbuf[i]
    lane1 = lax.broadcasted_iota(jnp.int32, (1, LANES), 1)
    chance_row = totals[GROUP:GROUP + 1, :]
    folded = chance_row
    for t in range(1, frames):
        folded = folded + pltpu.roll(chance_row, LANES - t, axis=1)
    count = jnp.sum(jnp.where(lane1 < frames, totals[GROUP + 3:GROUP + 4, :], 0.0))
    is_bit = (lane1 % frames == 0) & (lane1 < packed)
    marginal = jnp.where(is_bit, folded, 0.5 * count) / count
    terms = -marginal * jnp.log(marginal) - (1.0 - marginal) * jnp.log(1.0 - marginal)
    batch_entropy = jnp.sum(jnp.where(is_bit, terms, 0.0))
    entropy_sum = jnp.sum(totals[GROUP + 1:GROUP + 2, :])
    commit_sum = jnp.sum(totals[GROUP + 2:GROUP + 3, :])
    slots = 1.0 / float(rows * dp_count * frames * tm_count)
    penalty_ref[0, 0] = entropy_sum * slots - batch_entropy + 0.25 * commit_sum * slots

    for w in range(2):
        def first_sent(c, w=w):
            remote(
                group(w, c, major, 0, n - 1), p1_send.at[w], p1_recv.at[w], (right, tm)
            ).wait_send()
        on_core(first_sent)
        for step in range(1, last + 1):
            ring_sent(w, step)
        remote(wt.at[w, core], sib_send.at[w], sib_recv.at[w], (me, sibling)).wait_send()

    @pl.when(tm < tm_count - 1)
    def _():
        for k in range(CHUNKS):
            remote(leave.at[k], chain_send.at[k], chain_recv.at[k], (me, sibling)).wait_send()

    remote(arrived, a2a_send, a2a_recv, (right, tm)).wait_send()
    remote(
        tmbuf.at[pl.ds(0, tm_count - 1)], tm_send, tm_recv, (me, sibling)
    ).wait_send()


def shards(latents, lengths, plan, w_in, w_down, w_up, w_out, rate, gain, w_bits):
    rows, frames, width = latents.shape
    dp_count, tm_count = lax.axis_size("dp"), lax.axis_size("tm")
    n = math.isqrt(dp_count)
    bits = w_bits.shape[1]
    narrow_width = w_down.shape[1]
    part = rows // CHUNKS
    block = width // dp_count
    steps = n // 2
    vmem = pl.BlockSpec(memory_space=pltpu.VMEM)
    bf16, f32 = jnp.bfloat16, jnp.float32
    dma = pltpu.SemaphoreType.DMA
    codes, penalty = pl.pallas_call(
        functools.partial(kernel, dp_count, tm_count),
        out_shape=(
            jax.ShapeDtypeStruct((bits, frames, rows), bf16),
            jax.ShapeDtypeStruct((1, 1), f32),
        ),
        in_specs=[pl.BlockSpec(memory_space=pl.ANY)] + [vmem] * 9,
        out_specs=(vmem, pl.BlockSpec(memory_space=pltpu.SMEM)),
        scratch_shapes=[
            pltpu.VMEM((frames, rows, width), bf16),
            pltpu.VMEM((2, 2, n, n, block, width // 2), bf16),
            pltpu.VMEM((frames, rows, narrow_width), bf16),
            pltpu.VMEM((frames, rows, width), f32),
            pltpu.VMEM((frames, rows, width), f32),
            pltpu.VMEM((rows, width), f32),
            pltpu.VMEM((rows, width), f32),
            pltpu.VMEM((CHUNKS, part, width), bf16),
            pltpu.VMEM((CHUNKS, part, width), bf16),
            pltpu.VMEM((frames, part, width), bf16),
            pltpu.VMEM((frames * part, width), f32),
            pltpu.VMEM((frames, LANES, width), bf16),
            pltpu.VMEM((dp_count * 8, rows), bf16),
            pltpu.VMEM((dp_count * 8, rows), bf16),
            pltpu.VMEM((rows, LANES), f32),
            pltpu.VMEM((rows, LANES), f32),
            pltpu.VMEM((dp_count, 8, LANES), f32),
            pltpu.VMEM((dp_count, 8, LANES), f32),
            pltpu.VMEM((tm_count, 8, LANES), f32),
            dma,
            dma((2,)), dma((2,)),
            dma((2, 2, steps)), dma((2, 2, steps)),
            dma((2,)), dma((2,)),
            dma((CHUNKS,)), dma((CHUNKS,)),
            dma, dma, dma, dma,
        ],
        compiler_params=pltpu.CompilerParams(
            collective_id=0, has_side_effects=True, vmem_limit_bytes=56 * 1024 * 1024
        ),
    )(
        jnp.transpose(latents, (1, 0, 2)), lengths.reshape(1, rows), plan.reshape(1, rows),
        w_in.T, w_down.T, w_up, w_out.T, rate.reshape(1, width), gain.reshape(1, width), w_bits.T,
    )
    return codes, penalty[0, 0]


def solution(mesh):
    return jax.shard_map(
        shards,
        mesh=mesh,
        in_specs=(
            P("dp", "tm", None),
            P("dp"),
            P("dp"),
            P(None, "dp"),
            P(),
            P(),
            P(None, "dp"),
            P(),
            P(),
            P(),
        ),
        out_specs=(P(None, "tm", "dp"), P()),
        check_vma=False,
    )
```

```python
import functools
import math

import jax
import jax.numpy as jnp
from jax import lax
from jax.experimental import pallas as pl
from jax.experimental.pallas import tpu as pltpu
from jax.sharding import PartitionSpec as P

MESH = pl.DeviceIdType.MESH
GROUP = 4
LANES = 128
CHUNKS = 4
PIECES = 8
LOG2E = math.log2(math.e)


def nt(a, b):
    return lax.dot_general(a, b, (((1,), (1,)), ((), ())), preferred_element_type=jnp.float32)


def nn(a, b):
    return jnp.dot(a, b, preferred_element_type=jnp.float32)


def kernel(
    dp_count, tm_count, x_hbm, lengths_ref, plan_ref, win_ref, wdown_ref, wup_ref, wout_ref, rate_ref,
    gain_ref, wbits_ref, codes_ref, penalty_ref,
    x_ref, wt, narrow, dec, drv, reach, local, reach0, local0, ent, leave, enter, states, mixed, wb,
    onehot, pick, len_b, logits, sums, sendbuf, recvbuf, tmbuf,
    x_sem, p1_send, p1_recv, p2_send, p2_recv, xs_send, xs_recv, sib_send, sib_recv,
    reach_send, reach_recv, local_send, local_recv, chain_send, chain_recv, fwd_send,
    a2a_send, a2a_recv, tm_send, tm_recv,
):
    frames, rows, width = x_ref.shape
    n = math.isqrt(dp_count)
    quarter = width // 4
    part = rows // CHUNKS
    piece = rows // PIECES
    per_chunk = PIECES // CHUNKS
    tile = min(256, width)
    tiles = width // tile
    bits = wbits_ref.shape[0]
    packed = bits * frames
    chips = tm_count // 2
    me = lax.axis_index("dp")
    tm = lax.axis_index("tm")
    y, z = me // n, me % n
    chip, core = tm // 2, tm % 2
    odd = chip % 2
    major = y * (1 - core) + z * core
    minor = z * (1 - core) + y * core
    mine = 2 * core + odd
    other = 2 * core + 1 - odd
    sibling = tm + 1 - 2 * core
    next_chip = ((chip + 1) % chips) * 2 + core
    last_chip = ((chip + chips - 1) % chips) * 2 + core

    def dp_of(major_id, minor_id):
        return (major_id * n + minor_id) * (1 - core) + (minor_id * n + major_id) * core

    def on_core(make):
        pl.when(core == 0)(lambda: make(0))
        pl.when(core == 1)(lambda: make(1))

    offsets = [o for step in range(1, n // 2) for o in (step, -step)] + [n // 2]

    x_copy = pltpu.make_async_copy(x_hbm, x_ref, x_sem)
    x_copy.start()
    recvbuf[...] = jnp.zeros_like(recvbuf)

    barrier = pltpu.get_barrier_semaphore()

    def greet(dp_id, tm_id):
        pl.semaphore_signal(barrier, inc=1, device_id=(dp_id, tm_id), device_id_type=MESH)

    for step in range(1, n):
        greet(dp_of(major, (minor + step) % n), tm)
    for step in range(1, n):
        greet(dp_of((major + step) % n, minor), tm)
    for step in range(1, tm_count):
        greet(me, (tm + step) % tm_count)

    wt[0, mine, y, z] = win_ref[:, pl.ds(pl.multiple_of(mine * quarter, quarter), quarter)]
    for i in range(2):
        start = pl.multiple_of((2 * core + i) * quarter, quarter)
        wt[1, 2 * core + i, y, z] = wout_ref[:, pl.ds(start, quarter)]

    @pl.when(chip == 0)
    def _():
        ent[...] = jnp.zeros_like(ent)

    pl.semaphore_wait(barrier, 2 * (n - 1) + (tm_count - 1))

    def remote(ref, send, recv, device):
        return pltpu.make_async_remote_copy(
            src_ref=ref, dst_ref=ref, send_sem=send, recv_sem=recv,
            device_id=device, device_id_type=MESH,
        )

    firsts, counts = (mine, 2 * core), (1, 2)

    def group(w, c, major_id, first=None, low=0, count=n):
        quarters = pl.ds(firsts[w] if first is None else first, counts[w])
        if c == 0:
            return wt.at[w, quarters, major_id, pl.ds(low, count)]
        return wt.at[w, quarters, pl.ds(low, count), major_id]

    def group_id(position):
        return major if position == 0 else (major + 2 * n - offsets[position - 1]) % n

    def p1_start(w):
        for step in range(1, n):
            remote(
                wt.at[w, pl.ds(firsts[w], counts[w]), y, z], p1_send.at[w], p1_recv.at[w],
                (dp_of(major, (minor + step) % n), tm),
            ).start()

    def p1_all(w, c):
        return remote(
            group(w, c, major, None, 0, n - 1), p1_send.at[w], p1_recv.at[w], (me, sibling)
        )

    def p2_start(w):
        def make(c):
            p1_all(w, c).wait_recv()
            for i, offset in enumerate(offsets):
                remote(
                    group(w, c, major), p2_send.at[w], p2_recv.at[w, i],
                    (dp_of((major + offset + n) % n, minor), tm),
                ).start()
            forward(w, c, 0)
        on_core(make)

    def forward(w, c, position):
        held = group(w, c, group_id(position))
        if w == 0:
            target = next_chip if position % 2 == 0 else last_chip
            remote(held, xs_send, xs_recv.at[position], (me, target)).start()
        remote(held, sib_send.at[w], sib_recv.at[w], (me, sibling)).start()

    def p2_arrive(w, position):
        def make(c):
            remote(
                group(w, c, group_id(position)), p2_send.at[w], p2_recv.at[w, position - 1],
                (me, sibling),
            ).wait_recv()
            forward(w, c, position)
        on_core(make)

    def x_arrive(position):
        def make(c):
            held = group(0, c, group_id(position), other)
            remote(held, xs_send, xs_recv.at[position], (me, sibling)).wait_recv()
            remote(held, sib_send.at[0], sib_recv.at[0], (me, sibling)).start()
        on_core(make)

    def sibling_arrived(w):
        theirs = wt.at[w, pl.ds(2 * (1 - core), 2)]
        remote(theirs, sib_send.at[w], sib_recv.at[w], (me, sibling)).wait_recv()

    def small_things():
        first = tm * frames
        lengths = jnp.broadcast_to(lengths_ref[...].astype(jnp.float32), (LANES, rows))
        len_b[...] = lengths.T - first.astype(jnp.float32)
        spread = dp_count * 8
        slot = lax.broadcasted_iota(jnp.int32, (rows, spread), 1)
        source = lax.broadcasted_iota(jnp.int32, (rows, spread), 0)
        kept = slot % 8 < GROUP
        expand = jnp.where(kept & ((slot // 8) * GROUP + slot % 8 == source), 1.0, 0.0)
        expand = expand.astype(jnp.bfloat16)
        pick[...] = expand.T
        plan_rows = jnp.broadcast_to(plan_ref[...].astype(jnp.float32), (8, rows))
        wanted = nn(plan_rows.astype(jnp.bfloat16), expand)[0:1]
        chosen = jnp.where(kept & (wanted == source.astype(jnp.float32)), 1.0, 0.0)
        onehot[...] = chosen.T.astype(jnp.bfloat16)
        place = lax.broadcasted_iota(jnp.int32, (LANES, bits), 0)
        bit = lax.broadcasted_iota(jnp.int32, (LANES, bits), 1)
        for t in range(frames):
            chooser = jnp.where(place == bit + t * bits, 1.0, 0.0).astype(jnp.bfloat16)
            wb[t] = nn(chooser, wbits_ref[...]).astype(jnp.bfloat16)
        sums[...] = jnp.zeros_like(sums)

    def narrowing():
        x_copy.wait()
        for t in range(frames):
            narrow[t] = nt(x_ref[t], wdown_ref[...]).astype(jnp.bfloat16)

    def decays(t):
        for i in range(tiles):
            cols = slice(i * tile, (i + 1) * tile)
            u = nn(narrow[t], wup_ref[:, cols]) * LOG2E
            soft = jnp.maximum(u, 0.0) + jnp.log2(1.0 + jnp.exp2(-jnp.abs(u)))
            d = jnp.exp2(-rate_ref[:, cols] * soft)
            dec[t, :, cols] = d
            reach[:, cols] = d if t == 0 else reach[:, cols] * d

    def decay_frames(low, high):
        for t in range(low, min(high, frames)):
            decays(t)

    positions = len(offsets) + 1
    p1_start(0)
    narrowing()
    decay_frames(0, 1)
    p2_start(0)
    decay_frames(1, 3)
    x_done = 0
    for position in range(1, positions):
        p2_arrive(0, position)
        if position == 1:
            p1_start(1)
        if position == positions - 2 or positions == 2:
            p2_start(1)
        if position >= 4:
            x_arrive(x_done)
            x_done += 1
        if position == min(4, positions - 1):
            decay_frames(3, 4)
    decay_frames(4, 5)
    while x_done < positions - 2:
        x_arrive(x_done)
        x_done += 1
    decay_frames(5, frames)

    @pl.when(core == 0)
    def _():
        pltpu.make_async_remote_copy(
            src_ref=reach, dst_ref=reach0, send_sem=reach_send, recv_sem=reach_recv,
            device_id=(me, sibling), device_id_type=MESH,
        ).start()

    small_things()
    while x_done < positions:
        x_arrive(x_done)
        x_done += 1

    def weight_rows(w, i):
        per = n // tiles
        all_quarters = [wt[w, q, i * per:(i + 1) * per].reshape(tile, quarter) for q in range(4)]
        return jnp.concatenate(all_quarters, axis=1)

    def valid_of(k, t):
        rs = slice(k * part, (k + 1) * part)
        return jnp.where(len_b[rs, :] > float(t), 1.0, 0.0)

    def drives(k):
        rs = slice(k * part, (k + 1) * part)
        left_side = x_ref[:, rs, :].reshape(frames * part, width)
        for i in range(tiles):
            cols = slice(i * tile, (i + 1) * tile)
            pushed = nt(left_side, weight_rows(0, i)).reshape(frames, part, tile)
            running = None
            for t in range(frames):
                mask = jnp.concatenate([valid_of(k, t)] * max(1, tile // LANES), axis=1)[:, :tile]
                now = pushed[t] * mask
                drv[t, rs, cols] = now
                running = now if t == 0 else dec[t, rs, cols] * running + now
            local[rs, cols] = running

        @pl.when(core == 0)
        def _():
            pltpu.make_async_remote_copy(
                src_ref=local.at[pl.ds(k * part, part)], dst_ref=local0.at[pl.ds(k * part, part)],
                send_sem=local_send.at[k], recv_sem=local_recv.at[k],
                device_id=(me, sibling), device_id_type=MESH,
            ).start()

    def local_wait(k):
        remote(
            local0.at[pl.ds(k * part, part)], local_send.at[k], local_recv.at[k], (me, sibling)
        ).wait_recv()

    def reach_wait():
        remote(reach0, reach_send, reach_recv, (me, sibling)).wait_recv()

    def pass_on(j, sends=True, receives=True):
        rs = pl.ds(pl.multiple_of(j * piece, piece), piece)
        if receives:
            remote(ent.at[j], chain_send.at[j], chain_recv.at[j], (me, sibling)).wait_recv()
            remote(ent.at[j], fwd_send.at[j], chain_recv.at[j], (me, sibling)).start()
            between = reach0[rs, :] * ent[j].astype(jnp.float32) + local0[rs, :]
        else:
            between = local0[rs, :]
        enter[rs, :] = between
        if sends:
            leave[j] = (reach[rs, :] * between + local[rs, :]).astype(jnp.bfloat16)
            pltpu.make_async_remote_copy(
                src_ref=leave.at[j], dst_ref=ent.at[j],
                send_sem=chain_send.at[j], recv_sem=chain_recv.at[j],
                device_id=(me, next_chip), device_id_type=MESH,
            ).start()

    def pass_chunk(k, sends, receives):
        if k == 0:
            reach_wait()
        local_wait(k)
        for j in range(k * per_chunk, (k + 1) * per_chunk):
            pass_on(j, sends, receives)

    def pass_all():
        reach_wait()
        for k in range(CHUNKS):
            local_wait(k)

        def step(j, carry):
            pass_on(j)
            return carry

        lax.fori_loop(0, PIECES, step, 0)

    def outputs(k):
        rs = slice(k * part, (k + 1) * part)
        for i in range(tiles):
            cols = slice(i * tile, (i + 1) * tile)
            s = enter[rs, cols]
            for t in range(frames):
                s = dec[t, rs, cols] * s + drv[t, rs, cols]
                states[t, :, cols] = s.astype(jnp.bfloat16)
        left_side = states[...].reshape(frames * part, width)
        square = None
        for i in range(tiles):
            cols = slice(i * tile, (i + 1) * tile)
            x = x_ref[:, rs, cols].reshape(frames * part, tile).astype(jnp.float32)
            m = x + nt(left_side, weight_rows(1, i))
            mixed[:, cols] = m
            square = m * m if i == 0 else square + m * m
        scaling = lax.rsqrt(jnp.sum(square, axis=1, keepdims=True) * (1.0 / width) + 1e-06)
        values = None
        for t in range(frames):
            ts = slice(t * part, (t + 1) * part)
            normed = (mixed[ts, :] * scaling[ts, :] * gain_ref[...]).astype(jnp.bfloat16)
            term = nt(normed, wb[t])
            values = term if t == 0 else values + term
        logits[rs, :] = values.astype(jnp.bfloat16)
        lane = lax.broadcasted_iota(jnp.int32, (part, LANES), 1)
        frame = (lane // bits).astype(jnp.float32)
        weight = jnp.where((len_b[rs, :] > frame) & (lane < packed), 1.0, 0.0)
        scaled = 4.0 * values
        size = jnp.abs(scaled)
        e = jnp.exp(-size)
        inverse = 1.0 / (1.0 + e)
        chance = jnp.where(scaled >= 0.0, inverse, e * inverse)
        entropy = jnp.log(1.0 + e) + size * e * inverse
        commit = jnp.square(jnp.abs(values) - 1.0)
        for row, value in enumerate((chance, entropy, commit, None)):
            kept = weight if value is None else value * weight
            sums[row:row + 1, :] += jnp.sum(kept, axis=0, keepdims=True)

    is_core1 = core == 1
    sibling_arrived(0)
    for k in range(CHUNKS):
        drives(k)
        if k >= 1:
            @pl.when(is_core1 & (chip == 0))
            def _():
                pass_chunk(k - 1, True, False)

    @pl.when(is_core1 & (chip == 0))
    def _():
        pass_chunk(CHUNKS - 1, True, False)

    @pl.when(is_core1 & (chip == 1) & (chip < chips - 1))
    def _():
        pass_all()

    for position in range(1, positions):
        p2_arrive(1, position)

    @pl.when(is_core1 & (chip > 1) & (chip < chips - 1))
    def _():
        pass_all()

    sibling_arrived(1)
    for k in range(CHUNKS):
        @pl.when(is_core1 & (chip == chips - 1))
        def _():
            pass_chunk(k, False, True)

        @pl.when(core == 0)
        def _():
            for j in range(k * per_chunk, (k + 1) * per_chunk):
                @pl.when(chip > 0)
                def _():
                    remote(ent.at[j], fwd_send.at[j], chain_recv.at[j], (me, sibling)).wait_recv()

                enter[j * piece:(j + 1) * piece, :] = ent[j].astype(jnp.float32)

        outputs(k)

    folded = sums[...]
    folded = folded + pltpu.roll(folded, LANES - 3 * bits, axis=1)
    folded = (
        folded + pltpu.roll(folded, LANES - bits, axis=1)
        + pltpu.roll(folded, LANES - 2 * bits, axis=1)
    )
    riding = pltpu.roll(folded, packed, axis=1)
    lane8 = lax.broadcasted_iota(jnp.int32, (8, LANES), 1)
    riding = jnp.where((lane8 >= packed) & (lane8 < packed + bits), riding, 0.0)
    dealt = nn(onehot[...], logits[...])
    sendbuf[...] = dealt.reshape(dp_count, 8, LANES) + riding[None]
    recvbuf[me, 0:GROUP] = sendbuf[me, 0:GROUP]

    def deal(step, carry):
        peer = (me + step) % dp_count
        pltpu.make_async_remote_copy(
            src_ref=sendbuf.at[peer, pl.ds(0, GROUP)], dst_ref=recvbuf.at[me, pl.ds(0, GROUP)],
            send_sem=a2a_send, recv_sem=a2a_recv, device_id=(peer, tm), device_id_type=MESH,
        ).start()
        return carry

    lax.fori_loop(1, dp_count, deal, 0)
    arrived = remote(
        recvbuf.at[pl.ds(0, dp_count - 1), pl.ds(0, GROUP)], a2a_send, a2a_recv, (me, sibling)
    )
    arrived.wait_recv()

    tmbuf[tm] = jnp.sum(recvbuf[...], axis=0)
    for step in range(1, tm_count):
        remote(tmbuf.at[tm], tm_send, tm_recv, (me, (tm + step) % tm_count)).start()

    turned = recvbuf[...].reshape(dp_count * 8, LANES).T.astype(jnp.bfloat16)
    placed = nn(turned, pick[...])
    for t in range(frames):
        codes_ref[t] = placed[t * bits:(t + 1) * bits, :].astype(jnp.bfloat16)

    tm_all = remote(tmbuf.at[pl.ds(0, tm_count - 1)], tm_send, tm_recv, (me, sibling))
    tm_all.wait_recv()
    totals = tmbuf[0]
    for i in range(1, tm_count):
        totals = totals + tmbuf[i]
    lane1 = lax.broadcasted_iota(jnp.int32, (1, LANES), 1)
    is_bit = (lane1 >= packed) & (lane1 < packed + bits)
    marginal = jnp.where(is_bit, totals[0:1] / totals[3:4], 0.5)
    terms = -marginal * jnp.log(marginal) - (1.0 - marginal) * jnp.log(1.0 - marginal)
    slots = 1.0 / float(rows * dp_count * frames * tm_count)
    shares = (totals[1:2] + 0.25 * totals[2:3]) * slots - terms
    penalty_ref[0, 0] = jnp.sum(jnp.where(is_bit, shares, 0.0))

    def sent(c):
        for w in range(2):
            p1_all(w, c).wait_send()
            for i in range(len(offsets)):
                remote(
                    group(w, c, major), p2_send.at[w], p2_recv.at[w, i], (me, sibling)
                ).wait_send()

    on_core(sent)
    remote(wt.at[0, mine], xs_send, xs_recv.at[0], (me, sibling)).wait_send()
    for w in range(2):
        ours = wt.at[w, pl.ds(2 * core, 2)]
        remote(ours, sib_send.at[w], sib_recv.at[w], (me, sibling)).wait_send()

    @pl.when(core == 0)
    def _():
        remote(reach, reach_send, reach_recv, (me, sibling)).wait_send()
        for k in range(CHUNKS):
            remote(
                local.at[pl.ds(k * part, part)], local_send.at[k], local_recv.at[k], (me, sibling)
            ).wait_send()

    @pl.when(is_core1)
    def _():
        for j in range(PIECES):
            @pl.when(chip < chips - 1)
            def _():
                remote(leave.at[j], chain_send.at[j], chain_recv.at[j], (me, sibling)).wait_send()

            @pl.when(chip > 0)
            def _():
                remote(ent.at[j], fwd_send.at[j], chain_recv.at[j], (me, sibling)).wait_send()

    arrived.wait_send()
    tm_all.wait_send()


def shards(latents, lengths, plan, w_in, w_down, w_up, w_out, rate, gain, w_bits):
    rows, frames, width = latents.shape
    dp_count, tm_count = lax.axis_size("dp"), lax.axis_size("tm")
    n = math.isqrt(dp_count)
    bits = w_bits.shape[1]
    narrow_width = w_down.shape[1]
    part = rows // CHUNKS
    block = width // dp_count
    vmem = pl.BlockSpec(memory_space=pltpu.VMEM)
    bf16, f32 = jnp.bfloat16, jnp.float32
    dma = pltpu.SemaphoreType.DMA
    codes, penalty = pl.pallas_call(
        functools.partial(kernel, dp_count, tm_count),
        out_shape=(
            jax.ShapeDtypeStruct((frames, bits, rows), bf16),
            jax.ShapeDtypeStruct((1, 1), f32),
        ),
        in_specs=[pl.BlockSpec(memory_space=pl.ANY)] + [vmem] * 9,
        out_specs=(vmem, pl.BlockSpec(memory_space=pltpu.SMEM)),
        scratch_shapes=[
            pltpu.VMEM((frames, rows, width), bf16),
            pltpu.VMEM((2, 4, n, n, block, width // 4), bf16),
            pltpu.VMEM((frames, rows, narrow_width), bf16),
            pltpu.VMEM((frames, rows, width), f32),
            pltpu.VMEM((frames, rows, width), f32),
            pltpu.VMEM((rows, width), f32),
            pltpu.VMEM((rows, width), f32),
            pltpu.VMEM((rows, width), f32),
            pltpu.VMEM((rows, width), f32),
            pltpu.VMEM((PIECES, rows // PIECES, width), bf16),
            pltpu.VMEM((PIECES, rows // PIECES, width), bf16),
            pltpu.VMEM((rows, width), f32),
            pltpu.VMEM((frames, part, width), bf16),
            pltpu.VMEM((frames * part, width), f32),
            pltpu.VMEM((frames, LANES, width), bf16),
            pltpu.VMEM((dp_count * 8, rows), bf16),
            pltpu.VMEM((dp_count * 8, rows), bf16),
            pltpu.VMEM((rows, LANES), f32),
            pltpu.VMEM((rows, LANES), bf16),
            pltpu.VMEM((8, LANES), f32),
            pltpu.VMEM((dp_count, 8, LANES), f32),
            pltpu.VMEM((dp_count, 8, LANES), f32),
            pltpu.VMEM((tm_count, 8, LANES), f32),
            dma,
            dma((2,)), dma((2,)), dma((2,)), dma((2, n - 1)),
            dma, dma((n,)), dma((2,)), dma((2,)),
            dma, dma, dma((CHUNKS,)), dma((CHUNKS,)),
            dma((PIECES,)), dma((PIECES,)), dma((PIECES,)),
            dma, dma, dma, dma,
        ],
        compiler_params=pltpu.CompilerParams(
            collective_id=0, has_side_effects=True, vmem_limit_bytes=56 * 1024 * 1024
        ),
    )(
        jnp.transpose(latents, (1, 0, 2)), lengths.reshape(1, rows), plan.reshape(1, rows),
        w_in.T, w_down.T, w_up, w_out.T, rate.reshape(1, width), gain.reshape(1, width), w_bits.T,
    )
    return jnp.transpose(codes, (1, 0, 2)), penalty[0, 0]


def solution(mesh):
    return jax.shard_map(
        shards,
        mesh=mesh,
        in_specs=(
            P("dp", "tm", None),
            P("dp"),
            P("dp"),
            P(None, "dp"),
            P(),
            P(),
            P(None, "dp"),
            P(),
            P(),
            P(),
        ),
        out_specs=(P(None, "tm", "dp"), P()),
        check_vma=False,
    )
```

```python
import functools
import math

import jax
import jax.numpy as jnp
from jax import lax
from jax.experimental import pallas as pl
from jax.experimental.pallas import tpu as pltpu
from jax.sharding import PartitionSpec as P

MESH = pl.DeviceIdType.MESH
GROUP = 4
LANES = 128
CHUNKS = 4
PIECES = 8
LOG2E = math.log2(math.e)


def nt(a, b):
    return lax.dot_general(a, b, (((1,), (1,)), ((), ())), preferred_element_type=jnp.float32)


def nn(a, b):
    return jnp.dot(a, b, preferred_element_type=jnp.float32)


def kernel(
    dp_count, tm_count, x_hbm, *refs,
):
    smalls, refs = refs[:9], refs[9:]
    codes_ref, penalty_ref, *refs = refs
    lengths_ref, plan_ref, win_ref, wdown_ref, wup_ref, wout_ref, rate_ref, gain_ref, wbits_ref = refs[:9]
    small_sem, *refs = refs[9:]
    (
        x_ref, wt, narrow, dec, drv, reach, local, reach0, local0, ent, leave, enter, states, mixed, wb,
        onehot, pick, len_b, logits, sums, sendbuf, recvbuf, tmbuf,
        x_sem, p1_send, p1_recv, p2_send, p2_recv, xs_send, xs_recv, sib_send, sib_recv,
        reach_send, reach_recv, local_send, local_recv, chain_send, chain_recv, fwd_send,
        a2a_send, a2a_recv, tm_send, tm_recv,
    ) = refs
    frames, rows, width = x_ref.shape
    n = math.isqrt(dp_count)
    quarter = width // 4
    part = rows // CHUNKS
    piece = rows // PIECES
    per_chunk = PIECES // CHUNKS
    tile = min(256, width)
    tiles = width // tile
    bits = wbits_ref.shape[0]
    packed = bits * frames
    chips = tm_count // 2
    me = lax.axis_index("dp")
    tm = lax.axis_index("tm")
    y, z = me // n, me % n
    chip, core = tm // 2, tm % 2
    odd = chip % 2
    major = y * (1 - core) + z * core
    minor = z * (1 - core) + y * core
    mine = 2 * core + odd
    other = 2 * core + 1 - odd
    sibling = tm + 1 - 2 * core
    next_chip = ((chip + 1) % chips) * 2 + core
    last_chip = ((chip + chips - 1) % chips) * 2 + core

    def dp_of(major_id, minor_id):
        return (major_id * n + minor_id) * (1 - core) + (minor_id * n + major_id) * core

    def on_core(make):
        pl.when(core == 0)(lambda: make(0))
        pl.when(core == 1)(lambda: make(1))

    near = n // 4
    items = [(0, 0, n)]
    if n == 2:
        items += [(1, 0, n)]
    else:
        items += [(o, 0, n) for step in range(1, n // 2) for o in (-step, step)]
        items += [(n // 2, 0, n // 2), (n // 2, n // 2, n // 2)]
    early = 2 * near if n > 2 else 1

    x_copy = pltpu.make_async_copy(x_hbm, x_ref, x_sem)
    barrier = pltpu.get_barrier_semaphore()

    def greet(dp_id, tm_id):
        pl.semaphore_signal(barrier, inc=1, device_id=(dp_id, tm_id), device_id_type=MESH)

    for step in range(1, n):
        greet(dp_of(major, (minor + step) % n), tm)
    for step in range(1, n):
        greet(dp_of((major + step) % n, minor), tm)
    for step in range(1, tm_count):
        greet(me, (tm + step) % tm_count)

    small_copies = [
        pltpu.make_async_copy(source, target, small_sem.at[i])
        for i, (source, target) in enumerate(zip(smalls, (
            lengths_ref, plan_ref, win_ref, wdown_ref, wup_ref, wout_ref, rate_ref, gain_ref, wbits_ref
        )))
    ]
    for i in (2, 5, 3, 4, 6, 0, 1, 7, 8):
        small_copies[i].start()
    x_copy.start()
    small_copies[2].wait()
    small_copies[5].wait()

    wt[0, mine, y, z] = win_ref[:, pl.ds(pl.multiple_of(mine * quarter, quarter), quarter)]
    for i in range(2):
        start = pl.multiple_of((2 * core + i) * quarter, quarter)
        wt[1, 2 * core + i, y, z] = wout_ref[:, pl.ds(start, quarter)]

    @pl.when(chip == 0)
    def _():
        ent[...] = jnp.zeros_like(ent)

    recvbuf[...] = jnp.zeros_like(recvbuf)
    pl.semaphore_wait(barrier, 2 * (n - 1) + (tm_count - 1))

    def remote(ref, send, recv, device):
        return pltpu.make_async_remote_copy(
            src_ref=ref, dst_ref=ref, send_sem=send, recv_sem=recv,
            device_id=device, device_id_type=MESH,
        )

    firsts, counts = (mine, 2 * core), (1, 2)

    def group(w, c, major_id, first=None, low=0, count=n):
        quarters = pl.ds(firsts[w] if first is None else first, counts[w])
        if c == 0:
            return wt.at[w, quarters, major_id, pl.ds(low, count)]
        return wt.at[w, quarters, pl.ds(low, count), major_id]

    def at(offset):
        return (major + n + offset) % n

    def held(w, c, item, first=None):
        offset, low, count = items[item]
        return group(w, c, at(offset), first, low, count)

    def quarters_of(w):
        return pl.ds(firsts[w], counts[w])

    def p1_start(w):
        for step in range(1, n):
            remote(
                wt.at[w, quarters_of(w), y, z], p1_send.at[w], p1_recv.at[w],
                (dp_of(major, (minor + step) % n), tm),
            ).start()

    def p1_all(w):
        some = wt.at[w, quarters_of(w), 0, pl.ds(0, n - 1)]
        return remote(some, p1_send.at[w], p1_recv.at[w], (me, sibling))

    def p2_all(w):
        some = wt.at[w, quarters_of(w), pl.ds(0, n - 1)]
        return remote(some, p2_send.at[w], p2_recv.at[w, 0], (me, sibling))

    def send_group(w, piece_ref, item, toward):
        remote(
            piece_ref, p2_send.at[w], p2_recv.at[w, item - 1], (dp_of(at(toward), minor), tm)
        ).start()

    def near_sends(w):
        p1_all(w).wait_recv()

        def make(c):
            for item in range(1, early + 1):
                send_group(w, group(w, c, major), item, -items[item][0])
            forward(w, c, 0)
        on_core(make)

    def far_sends(w, c, item):
        offset = items[item][0]
        if n == 2 or item > early:
            return
        side = 1 if offset > 0 else -1
        if abs(offset) + near < n // 2:
            send_group(w, held(w, c, item), items.index((offset + side * near, 0, n)), -side * near)
        else:
            low = 0 if side < 0 else n // 2
            target = items.index((n // 2, low, n // 2))
            send_group(w, group(w, c, at(offset), None, low, n // 2), target, -side * near)

    def forward(w, c, item):
        if w == 0:
            target = next_chip if item % 2 == 0 and item < n - 1 else last_chip
            remote(held(w, c, item), xs_send, xs_recv.at[item], (me, target)).start()
        remote(held(w, c, item), sib_send.at[w], sib_recv.at[w], (me, sibling)).start()

    def arrive(w, item):
        def make(c):
            remote(
                held(w, c, item), p2_send.at[w], p2_recv.at[w, item - 1], (me, sibling)
            ).wait_recv()
            far_sends(w, c, item)
            forward(w, c, item)
        on_core(make)

    def x_arrive(item):
        def make(c):
            theirs = held(0, c, item, other)
            remote(theirs, xs_send, xs_recv.at[item], (me, sibling)).wait_recv()
            remote(theirs, sib_send.at[0], sib_recv.at[0], (me, sibling)).start()
        on_core(make)

    def sibling_arrived(w):
        theirs = wt.at[w, pl.ds(2 * (1 - core), 2)]
        remote(theirs, sib_send.at[w], sib_recv.at[w], (me, sibling)).wait_recv()

    def small_things():
        for i in (0, 1, 7, 8):
            small_copies[i].wait()
        first = tm * frames
        lengths = jnp.broadcast_to(lengths_ref[...].astype(jnp.float32), (LANES, rows))
        len_b[...] = lengths.T - first.astype(jnp.float32)
        spread = dp_count * 8
        slot = lax.broadcasted_iota(jnp.int32, (rows, spread), 1)
        source = lax.broadcasted_iota(jnp.int32, (rows, spread), 0)
        kept = slot % 8 < GROUP
        expand = jnp.where(kept & ((slot // 8) * GROUP + slot % 8 == source), 1.0, 0.0)
        expand = expand.astype(jnp.bfloat16)
        pick[...] = expand.T
        plan_rows = jnp.broadcast_to(plan_ref[...].astype(jnp.float32), (8, rows))
        wanted = nn(plan_rows.astype(jnp.bfloat16), expand)[0:1]
        chosen = jnp.where(kept & (wanted == source.astype(jnp.float32)), 1.0, 0.0)
        onehot[...] = chosen.T.astype(jnp.bfloat16)
        place = lax.broadcasted_iota(jnp.int32, (LANES, bits), 0)
        bit = lax.broadcasted_iota(jnp.int32, (LANES, bits), 1)
        for t in range(frames):
            chooser = jnp.where(place == bit + t * bits, 1.0, 0.0).astype(jnp.bfloat16)
            wb[t] = nn(chooser, wbits_ref[...]).astype(jnp.bfloat16)
        sums[...] = jnp.zeros_like(sums)

    def narrowing():
        for i in (3, 4, 6):
            small_copies[i].wait()
        x_copy.wait()
        for t in range(frames):
            narrow[t] = nt(x_ref[t], wdown_ref[...]).astype(jnp.bfloat16)

    def decays(t):
        for i in range(tiles):
            cols = slice(i * tile, (i + 1) * tile)
            u = nn(narrow[t], wup_ref[:, cols]) * LOG2E
            soft = jnp.maximum(u, 0.0) + jnp.log2(1.0 + jnp.exp2(-jnp.abs(u)))
            d = jnp.exp2(-rate_ref[:, cols] * soft)
            dec[t, :, cols] = d
            reach[:, cols] = d if t == 0 else reach[:, cols] * d

    def decay_frames(low, high):
        for t in range(low, min(high, frames)):
            decays(t)

    count = len(items)
    p1_start(0)
    narrowing()
    decay_frames(0, 1)
    near_sends(0)
    p1_start(1)
    decay_frames(1, 3)
    for item in range(1, early + 1):
        arrive(0, item)
    near_sends(1)
    decay_frames(3, 4)
    x_done = 0
    for item in range(early + 1, count):
        x_arrive(x_done)
        x_done += 1
        arrive(0, item)
    decay_frames(4, frames)

    @pl.when(core == 0)
    def _():
        pltpu.make_async_remote_copy(
            src_ref=reach, dst_ref=reach0, send_sem=reach_send, recv_sem=reach_recv,
            device_id=(me, sibling), device_id_type=MESH,
        ).start()

    small_things()
    while x_done < count:
        x_arrive(x_done)
        x_done += 1

    def weight_rows(w, i):
        per = n // tiles
        all_quarters = [wt[w, q, i * per:(i + 1) * per].reshape(tile, quarter) for q in range(4)]
        return jnp.concatenate(all_quarters, axis=1)

    def valid_of(k, t):
        rs = slice(k * part, (k + 1) * part)
        return jnp.where(len_b[rs, :] > float(t), 1.0, 0.0)

    def drives(k):
        rs = slice(k * part, (k + 1) * part)
        left_side = x_ref[:, rs, :].reshape(frames * part, width)
        for i in range(tiles):
            cols = slice(i * tile, (i + 1) * tile)
            pushed = nt(left_side, weight_rows(0, i)).reshape(frames, part, tile)
            running = None
            for t in range(frames):
                mask = jnp.concatenate([valid_of(k, t)] * max(1, tile // LANES), axis=1)[:, :tile]
                now = pushed[t] * mask
                drv[t, rs, cols] = now
                running = now if t == 0 else dec[t, rs, cols] * running + now
            local[rs, cols] = running

        @pl.when(core == 0)
        def _():
            pltpu.make_async_remote_copy(
                src_ref=local.at[pl.ds(k * part, part)], dst_ref=local0.at[pl.ds(k * part, part)],
                send_sem=local_send.at[k], recv_sem=local_recv.at[k],
                device_id=(me, sibling), device_id_type=MESH,
            ).start()

    def local_wait(k):
        remote(
            local0.at[pl.ds(k * part, part)], local_send.at[k], local_recv.at[k], (me, sibling)
        ).wait_recv()

    def reach_wait():
        remote(reach0, reach_send, reach_recv, (me, sibling)).wait_recv()

    def pass_on(j, sends=True, receives=True):
        rs = pl.ds(pl.multiple_of(j * piece, piece), piece)
        if receives:
            remote(ent.at[j], chain_send.at[j], chain_recv.at[j], (me, sibling)).wait_recv()
            remote(ent.at[j], fwd_send.at[j], chain_recv.at[j], (me, sibling)).start()
            between = reach0[rs, :] * ent[j].astype(jnp.float32) + local0[rs, :]
        else:
            between = local0[rs, :]
        enter[rs, :] = between
        if sends:
            leave[j] = (reach[rs, :] * between + local[rs, :]).astype(jnp.bfloat16)
            pltpu.make_async_remote_copy(
                src_ref=leave.at[j], dst_ref=ent.at[j],
                send_sem=chain_send.at[j], recv_sem=chain_recv.at[j],
                device_id=(me, next_chip), device_id_type=MESH,
            ).start()

    def pass_chunk(k, sends, receives):
        if k == 0:
            reach_wait()
        local_wait(k)
        for j in range(k * per_chunk, (k + 1) * per_chunk):
            pass_on(j, sends, receives)

    def pass_all():
        reach_wait()
        for k in range(CHUNKS):
            local_wait(k)

        def step(j, carry):
            pass_on(j)
            return carry

        lax.fori_loop(0, PIECES, step, 0)

    def outputs(k):
        rs = slice(k * part, (k + 1) * part)
        for i in range(tiles):
            cols = slice(i * tile, (i + 1) * tile)
            s = enter[rs, cols]
            for t in range(frames):
                s = dec[t, rs, cols] * s + drv[t, rs, cols]
                states[t, :, cols] = s.astype(jnp.bfloat16)
        left_side = states[...].reshape(frames * part, width)
        square = None
        for i in range(tiles):
            cols = slice(i * tile, (i + 1) * tile)
            x = x_ref[:, rs, cols].reshape(frames * part, tile).astype(jnp.float32)
            m = x + nt(left_side, weight_rows(1, i))
            mixed[:, cols] = m
            square = m * m if i == 0 else square + m * m
        scaling = lax.rsqrt(jnp.sum(square, axis=1, keepdims=True) * (1.0 / width) + 1e-06)
        values = None
        for t in range(frames):
            ts = slice(t * part, (t + 1) * part)
            normed = (mixed[ts, :] * scaling[ts, :] * gain_ref[...]).astype(jnp.bfloat16)
            term = nt(normed, wb[t])
            values = term if t == 0 else values + term
        logits[rs, :] = values.astype(jnp.bfloat16)
        lane = lax.broadcasted_iota(jnp.int32, (part, LANES), 1)
        frame = (lane // bits).astype(jnp.float32)
        weight = jnp.where((len_b[rs, :] > frame) & (lane < packed), 1.0, 0.0)
        scaled = 4.0 * values
        size = jnp.abs(scaled)
        e = jnp.exp(-size)
        inverse = 1.0 / (1.0 + e)
        chance = jnp.where(scaled >= 0.0, inverse, e * inverse)
        entropy = jnp.log(1.0 + e) + size * e * inverse
        commit = jnp.square(jnp.abs(values) - 1.0)
        for row, value in enumerate((chance, entropy, commit, None)):
            kept = weight if value is None else value * weight
            sums[row:row + 1, :] += jnp.sum(kept, axis=0, keepdims=True)

    is_core1 = core == 1
    sibling_arrived(0)
    for k in range(CHUNKS):
        drives(k)
        if k >= 1:
            @pl.when(is_core1 & (chip == 0))
            def _():
                pass_chunk(k - 1, True, False)
        if k == 0:
            for item in range(1, early + 1):
                arrive(1, item)

    @pl.when(is_core1 & (chip == 0))
    def _():
        pass_chunk(CHUNKS - 1, True, False)

    @pl.when(is_core1 & (chip == 1) & (chip < chips - 1))
    def _():
        pass_all()

    for item in range(early + 1, count):
        arrive(1, item)

    @pl.when(is_core1 & (chip > 1) & (chip < chips - 1))
    def _():
        pass_all()

    sibling_arrived(1)
    for k in range(CHUNKS):
        @pl.when(is_core1 & (chip == chips - 1))
        def _():
            pass_chunk(k, False, True)

        @pl.when(core == 0)
        def _():
            for j in range(k * per_chunk, (k + 1) * per_chunk):
                @pl.when(chip > 0)
                def _():
                    remote(ent.at[j], fwd_send.at[j], chain_recv.at[j], (me, sibling)).wait_recv()

                enter[j * piece:(j + 1) * piece, :] = ent[j].astype(jnp.float32)

        outputs(k)

    folded = sums[...]
    folded = folded + pltpu.roll(folded, LANES - 3 * bits, axis=1)
    folded = (
        folded + pltpu.roll(folded, LANES - bits, axis=1)
        + pltpu.roll(folded, LANES - 2 * bits, axis=1)
    )
    riding = pltpu.roll(folded, packed, axis=1)
    lane8 = lax.broadcasted_iota(jnp.int32, (8, LANES), 1)
    riding = jnp.where((lane8 >= packed) & (lane8 < packed + bits), riding, 0.0)
    dealt = nn(onehot[...], logits[...])
    sendbuf[...] = dealt.reshape(dp_count, 8, LANES) + riding[None]
    recvbuf[me, 0:GROUP] = sendbuf[me, 0:GROUP]

    def from_far(i):
        return n // 2 + (i // 2) * (1 - 2 * (i % 2)) - i % 2

    def deal(step):
        peer = (y + from_far(step // n)) % n * n + (z + from_far(step % n)) % n
        pltpu.make_async_remote_copy(
            src_ref=sendbuf.at[peer, pl.ds(0, GROUP)], dst_ref=recvbuf.at[me, pl.ds(0, GROUP)],
            send_sem=a2a_send, recv_sem=a2a_recv, device_id=(peer, tm), device_id_type=MESH,
        ).start()

    unrolled = 3 if (dp_count - 1) % 3 == 0 else 1

    def deal_some(i, carry):
        for j in range(unrolled):
            deal(i * unrolled + j)
        return carry

    lax.fori_loop(0, (dp_count - 1) // unrolled, deal_some, 0)

    for w in range(2):
        p1_all(w).wait_send()
        p2_all(w).wait_send()
        ours = wt.at[w, pl.ds(2 * core, 2)]
        remote(ours, sib_send.at[w], sib_recv.at[w], (me, sibling)).wait_send()
    remote(wt.at[0, mine], xs_send, xs_recv.at[0], (me, sibling)).wait_send()

    @pl.when(core == 0)
    def _():
        remote(reach, reach_send, reach_recv, (me, sibling)).wait_send()
        for k in range(CHUNKS):
            remote(
                local.at[pl.ds(k * part, part)], local_send.at[k], local_recv.at[k], (me, sibling)
            ).wait_send()

    @pl.when(is_core1)
    def _():
        for j in range(PIECES):
            @pl.when(chip < chips - 1)
            def _():
                remote(leave.at[j], chain_send.at[j], chain_recv.at[j], (me, sibling)).wait_send()

            @pl.when(chip > 0)
            def _():
                remote(ent.at[j], fwd_send.at[j], chain_recv.at[j], (me, sibling)).wait_send()

    arrived = remote(
        recvbuf.at[pl.ds(0, dp_count - 1), pl.ds(0, GROUP)], a2a_send, a2a_recv, (me, sibling)
    )
    arrived.wait_recv()

    tmbuf[tm] = jnp.sum(recvbuf[...], axis=0)
    for step in range(1, tm_count):
        remote(tmbuf.at[tm], tm_send, tm_recv, (me, (tm + step) % tm_count)).start()

    turned = recvbuf[...].reshape(dp_count * 8, LANES).T.astype(jnp.bfloat16)
    placed = nn(turned, pick[...])
    for t in range(frames):
        codes_ref[t] = placed[t * bits:(t + 1) * bits, :].astype(jnp.bfloat16)

    tm_all = remote(tmbuf.at[pl.ds(0, tm_count - 1)], tm_send, tm_recv, (me, sibling))
    tm_all.wait_recv()
    totals = tmbuf[0]
    for i in range(1, tm_count):
        totals = totals + tmbuf[i]
    lane1 = lax.broadcasted_iota(jnp.int32, (1, LANES), 1)
    is_bit = (lane1 >= packed) & (lane1 < packed + bits)
    marginal = jnp.where(is_bit, totals[0:1] / totals[3:4], 0.5)
    terms = -marginal * jnp.log(marginal) - (1.0 - marginal) * jnp.log(1.0 - marginal)
    slots = 1.0 / float(rows * dp_count * frames * tm_count)
    shares = (totals[1:2] + 0.25 * totals[2:3]) * slots - terms
    penalty_ref[0, 0] = jnp.sum(jnp.where(is_bit, shares, 0.0))

    arrived.wait_send()
    tm_all.wait_send()


def shards(latents, lengths, plan, w_in, w_down, w_up, w_out, rate, gain, w_bits):
    rows, frames, width = latents.shape
    dp_count, tm_count = lax.axis_size("dp"), lax.axis_size("tm")
    n = math.isqrt(dp_count)
    bits = w_bits.shape[1]
    narrow_width = w_down.shape[1]
    part = rows // CHUNKS
    block = width // dp_count
    vmem = pl.BlockSpec(memory_space=pltpu.VMEM)
    bf16, f32 = jnp.bfloat16, jnp.float32
    dma = pltpu.SemaphoreType.DMA
    codes, penalty = pl.pallas_call(
        functools.partial(kernel, dp_count, tm_count),
        out_shape=(
            jax.ShapeDtypeStruct((frames, bits, rows), bf16),
            jax.ShapeDtypeStruct((1, 1), f32),
        ),
        in_specs=[pl.BlockSpec(memory_space=pl.ANY)] * 10,
        out_specs=(vmem, pl.BlockSpec(memory_space=pltpu.SMEM)),
        scratch_shapes=[
            pltpu.VMEM((1, rows), jnp.int32),
            pltpu.VMEM((1, rows), jnp.int32),
            pltpu.VMEM((block, width), bf16),
            pltpu.VMEM((narrow_width, width), bf16),
            pltpu.VMEM((narrow_width, width), bf16),
            pltpu.VMEM((block, width), bf16),
            pltpu.VMEM((1, width), f32),
            pltpu.VMEM((1, width), f32),
            pltpu.VMEM((bits, width), bf16),
            dma((9,)),
            pltpu.VMEM((frames, rows, width), bf16),
            pltpu.VMEM((2, 4, n, n, block, width // 4), bf16),
            pltpu.VMEM((frames, rows, narrow_width), bf16),
            pltpu.VMEM((frames, rows, width), f32),
            pltpu.VMEM((frames, rows, width), f32),
            pltpu.VMEM((rows, width), f32),
            pltpu.VMEM((rows, width), f32),
            pltpu.VMEM((rows, width), f32),
            pltpu.VMEM((rows, width), f32),
            pltpu.VMEM((PIECES, rows // PIECES, width), bf16),
            pltpu.VMEM((PIECES, rows // PIECES, width), bf16),
            pltpu.VMEM((rows, width), f32),
            pltpu.VMEM((frames, part, width), bf16),
            pltpu.VMEM((frames * part, width), f32),
            pltpu.VMEM((frames, LANES, width), bf16),
            pltpu.VMEM((dp_count * 8, rows), bf16),
            pltpu.VMEM((dp_count * 8, rows), bf16),
            pltpu.VMEM((rows, LANES), f32),
            pltpu.VMEM((rows, LANES), bf16),
            pltpu.VMEM((8, LANES), f32),
            pltpu.VMEM((dp_count, 8, LANES), f32),
            pltpu.VMEM((dp_count, 8, LANES), f32),
            pltpu.VMEM((tm_count, 8, LANES), f32),
            dma,
            dma((2,)), dma((2,)), dma((2,)), dma((2, n)),
            dma, dma((n + 1,)), dma((2,)), dma((2,)),
            dma, dma, dma((CHUNKS,)), dma((CHUNKS,)),
            dma((PIECES,)), dma((PIECES,)), dma((PIECES,)),
            dma, dma, dma, dma,
        ],
        compiler_params=pltpu.CompilerParams(
            collective_id=0, has_side_effects=True, vmem_limit_bytes=56 * 1024 * 1024
        ),
    )(
        jnp.transpose(latents, (1, 0, 2)), lengths.reshape(1, rows), plan.reshape(1, rows),
        w_in.T, w_down.T, w_up, w_out.T, rate.reshape(1, width), gain.reshape(1, width), w_bits.T,
    )
    return jnp.transpose(codes, (1, 0, 2)), penalty[0, 0]


def solution(mesh):
    return jax.shard_map(
        shards,
        mesh=mesh,
        in_specs=(
            P("dp", "tm", None),
            P("dp"),
            P("dp"),
            P(None, "dp"),
            P(),
            P(),
            P(None, "dp"),
            P(),
            P(),
            P(),
        ),
        out_specs=(P(None, "tm", "dp"), P()),
        check_vma=False,
    )
```

```python
import functools
import math

import jax
import jax.numpy as jnp
from jax import lax
from jax.experimental import pallas as pl
from jax.experimental.pallas import tpu as pltpu
from jax.sharding import PartitionSpec as P

MESH = pl.DeviceIdType.MESH
GROUP = 4
LANES = 128
CHUNKS = 4
PIECES = 16
LOG2E = math.log2(math.e)


def nt(a, b):
    return lax.dot_general(a, b, (((1,), (1,)), ((), ())), preferred_element_type=jnp.float32)


def nn(a, b):
    return jnp.dot(a, b, preferred_element_type=jnp.float32)


def kernel(
    dp_count, tm_count, x_hbm, *refs,
):
    smalls, refs = refs[:9], refs[9:]
    codes_ref, penalty_ref, *refs = refs
    lengths_ref, plan_ref, win_ref, wdown_ref, wup_ref, wout_ref, rate_ref, gain_ref, wbits_ref = refs[:9]
    small_sem, *refs = refs[9:]
    (
        x_ref, wt, narrow, dec, drv, reach, local, reach0, local0, ent, leave, enter, states, mixed, wb,
        onehot, pick, len_b, logits, sums, sendbuf, recvbuf, tmbuf, zbuf, ybuf, staged,
        x_sem, p1_send, p1_recv, p2_send, p2_recv, xs_send, xs_recv, sib_send, sib_recv,
        reach_send, reach_recv, local_send, local_recv, chain_send, chain_recv, fwd_send,
        a2a_send, a2a_recv, sum_send, sum_recv, store_sem,
    ) = refs
    frames, rows, width = x_ref.shape
    n = math.isqrt(dp_count)
    quarter = width // 4
    part = rows // CHUNKS
    piece = rows // PIECES
    per_chunk = PIECES // CHUNKS
    tile = min(256, width)
    tiles = width // tile
    bits = wbits_ref.shape[0]
    packed = bits * frames
    chips = tm_count // 2
    me = lax.axis_index("dp")
    tm = lax.axis_index("tm")
    y, z = me // n, me % n
    chip, core = tm // 2, tm % 2
    odd = chip % 2
    major = y * (1 - core) + z * core
    minor = z * (1 - core) + y * core
    mine = 2 * core + odd
    other = 2 * core + 1 - odd
    sibling = tm + 1 - 2 * core
    next_chip = ((chip + 1) % chips) * 2 + core
    last_chip = ((chip + chips - 1) % chips) * 2 + core

    def dp_of(major_id, minor_id):
        return (major_id * n + minor_id) * (1 - core) + (minor_id * n + major_id) * core

    def on_core(make):
        pl.when(core == 0)(lambda: make(0))
        pl.when(core == 1)(lambda: make(1))

    near = n // 4
    items = [(0, 0, n)]
    if n == 2:
        items += [(1, 0, n)]
    else:
        items += [(o, 0, n) for step in range(1, n // 2) for o in (-step, step)]
        items += [(n // 2, 0, n // 2), (n // 2, n // 2, n // 2)]
    early = 2 * near if n > 2 else 1

    x_copy = pltpu.make_async_copy(x_hbm, x_ref, x_sem)
    barrier = pltpu.get_barrier_semaphore()

    def greet(dp_id, tm_id):
        pl.semaphore_signal(barrier, inc=1, device_id=(dp_id, tm_id), device_id_type=MESH)

    for step in range(1, n):
        greet(dp_of(major, (minor + step) % n), tm)
    for step in range(1, n):
        greet(dp_of((major + step) % n, minor), tm)
    for step in range(1, tm_count):
        greet(me, (tm + step) % tm_count)

    small_copies = [
        pltpu.make_async_copy(source, target, small_sem.at[i])
        for i, (source, target) in enumerate(zip(smalls, (
            lengths_ref, plan_ref, win_ref, wdown_ref, wup_ref, wout_ref, rate_ref, gain_ref, wbits_ref
        )))
    ]
    for i in (2, 5, 3, 4, 6, 0, 1, 7, 8):
        small_copies[i].start()
    x_copy.start()
    small_copies[2].wait()
    small_copies[5].wait()

    wt[0, mine, y, z] = win_ref[:, pl.ds(pl.multiple_of(mine * quarter, quarter), quarter)]
    for i in range(2):
        start = pl.multiple_of((2 * core + i) * quarter, quarter)
        wt[1, 2 * core + i, y, z] = wout_ref[:, pl.ds(start, quarter)]

    @pl.when(chip == 0)
    def _():
        ent[...] = jnp.zeros_like(ent)

    recvbuf[...] = jnp.zeros_like(recvbuf)
    pl.semaphore_wait(barrier, 2 * (n - 1) + (tm_count - 1))

    def remote(ref, send, recv, device):
        return pltpu.make_async_remote_copy(
            src_ref=ref, dst_ref=ref, send_sem=send, recv_sem=recv,
            device_id=device, device_id_type=MESH,
        )

    firsts, counts = (mine, 2 * core), (1, 2)

    def group(w, c, major_id, first=None, low=0, count=n):
        quarters = pl.ds(firsts[w] if first is None else first, counts[w])
        if c == 0:
            return wt.at[w, quarters, major_id, pl.ds(low, count)]
        return wt.at[w, quarters, pl.ds(low, count), major_id]

    def at(offset):
        return (major + n + offset) % n

    def held(w, c, item, first=None):
        offset, low, count = items[item]
        return group(w, c, at(offset), first, low, count)

    def quarters_of(w):
        return pl.ds(firsts[w], counts[w])

    def p1_start(w):
        for step in range(1, n):
            remote(
                wt.at[w, quarters_of(w), y, z], p1_send.at[w], p1_recv.at[w],
                (dp_of(major, (minor + step) % n), tm),
            ).start()

    def p1_all(w):
        some = wt.at[w, quarters_of(w), 0, pl.ds(0, n - 1)]
        return remote(some, p1_send.at[w], p1_recv.at[w], (me, sibling))

    def p2_all(w):
        some = wt.at[w, quarters_of(w), pl.ds(0, n - 1)]
        return remote(some, p2_send.at[w], p2_recv.at[w, 0], (me, sibling))

    def send_group(w, piece_ref, item, toward):
        remote(
            piece_ref, p2_send.at[w], p2_recv.at[w, item - 1], (dp_of(at(toward), minor), tm)
        ).start()

    def near_sends(w):
        p1_all(w).wait_recv()

        def make(c):
            for item in range(1, early + 1):
                send_group(w, group(w, c, major), item, -items[item][0])
            forward(w, c, 0)
        on_core(make)

    def far_sends(w, c, item):
        offset = items[item][0]
        if n == 2 or item > early:
            return
        side = 1 if offset > 0 else -1
        if abs(offset) + near < n // 2:
            send_group(w, held(w, c, item), items.index((offset + side * near, 0, n)), -side * near)
        else:
            low = 0 if side < 0 else n // 2
            target = items.index((n // 2, low, n // 2))
            send_group(w, group(w, c, at(offset), None, low, n // 2), target, -side * near)

    def forward(w, c, item):
        if w == 0:
            target = next_chip if item % 2 == 0 and item < n - 1 else last_chip
            remote(held(w, c, item), xs_send, xs_recv.at[item], (me, target)).start()
        remote(held(w, c, item), sib_send.at[w], sib_recv.at[w], (me, sibling)).start()

    def arrive(w, item):
        def make(c):
            remote(
                held(w, c, item), p2_send.at[w], p2_recv.at[w, item - 1], (me, sibling)
            ).wait_recv()
            far_sends(w, c, item)
            forward(w, c, item)
        on_core(make)

    def x_arrive(item):
        def make(c):
            theirs = held(0, c, item, other)
            remote(theirs, xs_send, xs_recv.at[item], (me, sibling)).wait_recv()
            remote(theirs, sib_send.at[0], sib_recv.at[0], (me, sibling)).start()
        on_core(make)

    def sibling_arrived(w):
        theirs = wt.at[w, pl.ds(2 * (1 - core), 2)]
        remote(theirs, sib_send.at[w], sib_recv.at[w], (me, sibling)).wait_recv()

    def small_things():
        for i in (0, 1, 7, 8):
            small_copies[i].wait()
        first = tm * frames
        lengths = jnp.broadcast_to(lengths_ref[...].astype(jnp.float32), (LANES, rows))
        len_b[...] = lengths.T - first.astype(jnp.float32)
        spread = dp_count * 8
        slot = lax.broadcasted_iota(jnp.int32, (rows, spread), 1)
        source = lax.broadcasted_iota(jnp.int32, (rows, spread), 0)
        kept = slot % 8 < GROUP
        expand = jnp.where(kept & ((slot // 8) * GROUP + slot % 8 == source), 1.0, 0.0)
        expand = expand.astype(jnp.bfloat16)
        pick[...] = expand.T
        plan_rows = jnp.broadcast_to(plan_ref[...].astype(jnp.float32), (8, rows))
        wanted = nn(plan_rows.astype(jnp.bfloat16), expand)[0:1]
        chosen = jnp.where(kept & (wanted == source.astype(jnp.float32)), 1.0, 0.0)
        onehot[...] = chosen.T.astype(jnp.bfloat16)
        place = lax.broadcasted_iota(jnp.int32, (LANES, bits), 0)
        bit = lax.broadcasted_iota(jnp.int32, (LANES, bits), 1)
        chooser = jnp.where(place == bit, 1.0, 0.0).astype(jnp.bfloat16)
        wb[...] = nn(chooser, wbits_ref[...]).astype(jnp.bfloat16)
        sums[...] = jnp.zeros_like(sums)

    def narrowing():
        for i in (3, 4, 6):
            small_copies[i].wait()
        x_copy.wait()
        for t in range(frames):
            narrow[t] = nt(x_ref[t], wdown_ref[...]).astype(jnp.bfloat16)

    def decays(t):
        for i in range(tiles):
            cols = slice(i * tile, (i + 1) * tile)
            u = nn(narrow[t], wup_ref[:, cols]) * LOG2E
            soft = jnp.maximum(u, 0.0) + jnp.log2(1.0 + jnp.exp2(-jnp.abs(u)))
            d = jnp.exp2(-rate_ref[:, cols] * soft)
            dec[t, :, cols] = d
            reach[:, cols] = d if t == 0 else reach[:, cols] * d

    def decay_frames(low, high):
        for t in range(low, min(high, frames)):
            decays(t)

    count = len(items)
    p1_start(0)
    narrowing()
    decay_frames(0, 1)
    near_sends(0)
    p1_start(1)
    decay_frames(1, 3)
    for item in range(1, early + 1):
        arrive(0, item)
    near_sends(1)
    decay_frames(3, 4)
    x_done = 0
    for item in range(early + 1, count):
        x_arrive(x_done)
        x_done += 1
        arrive(0, item)
    decay_frames(4, frames)

    @pl.when(core == 0)
    def _():
        pltpu.make_async_remote_copy(
            src_ref=reach, dst_ref=reach0, send_sem=reach_send, recv_sem=reach_recv,
            device_id=(me, sibling), device_id_type=MESH,
        ).start()

    small_things()
    while x_done < count:
        x_arrive(x_done)
        x_done += 1

    def weight_rows(w, i):
        per = n // tiles
        all_quarters = [wt[w, q, i * per:(i + 1) * per].reshape(tile, quarter) for q in range(4)]
        return jnp.concatenate(all_quarters, axis=1)

    def valid_of(k, t):
        rs = slice(k * part, (k + 1) * part)
        return jnp.where(len_b[rs, :] > float(t), 1.0, 0.0)

    def drives(k):
        rs = slice(k * part, (k + 1) * part)
        left_side = x_ref[:, rs, :].reshape(frames * part, width)
        for i in range(tiles):
            cols = slice(i * tile, (i + 1) * tile)
            pushed = nt(left_side, weight_rows(0, i)).reshape(frames, part, tile)
            running = None
            for t in range(frames):
                mask = jnp.concatenate([valid_of(k, t)] * max(1, tile // LANES), axis=1)[:, :tile]
                now = pushed[t] * mask
                drv[t, rs, cols] = now
                running = now if t == 0 else dec[t, rs, cols] * running + now
            local[rs, cols] = running

        @pl.when(core == 0)
        def _():
            pltpu.make_async_remote_copy(
                src_ref=local.at[pl.ds(k * part, part)], dst_ref=local0.at[pl.ds(k * part, part)],
                send_sem=local_send.at[k], recv_sem=local_recv.at[k],
                device_id=(me, sibling), device_id_type=MESH,
            ).start()

    def local_wait(k):
        remote(
            local0.at[pl.ds(k * part, part)], local_send.at[k], local_recv.at[k], (me, sibling)
        ).wait_recv()

    def reach_wait():
        remote(reach0, reach_send, reach_recv, (me, sibling)).wait_recv()

    def pass_on(j, sends=True, receives=True):
        rs = pl.ds(pl.multiple_of(j * piece, piece), piece)
        if receives:
            remote(ent.at[j], chain_send.at[j], chain_recv.at[j], (me, sibling)).wait_recv()
            remote(ent.at[j], fwd_send.at[j], chain_recv.at[j], (me, sibling)).start()
            between = reach0[rs, :] * ent[j].astype(jnp.float32) + local0[rs, :]
        else:
            between = local0[rs, :]
        enter[rs, :] = between
        if sends:
            leave[j] = (reach[rs, :] * between + local[rs, :]).astype(jnp.bfloat16)
            pltpu.make_async_remote_copy(
                src_ref=leave.at[j], dst_ref=ent.at[j],
                send_sem=chain_send.at[j], recv_sem=chain_recv.at[j],
                device_id=(me, next_chip), device_id_type=MESH,
            ).start()

    def pass_chunk(k, sends, receives):
        if k == 0:
            reach_wait()
        local_wait(k)
        for j in range(k * per_chunk, (k + 1) * per_chunk):
            pass_on(j, sends, receives)

    def pass_half(h):
        if h == 0:
            reach_wait()
        for k in range(h * CHUNKS // 2, (h + 1) * CHUNKS // 2):
            local_wait(k)

        def step(j, carry):
            pass_on(j)
            return carry

        lax.fori_loop(h * PIECES // 2, (h + 1) * PIECES // 2, step, 0)

    def outputs(k):
        rs = slice(k * part, (k + 1) * part)
        for i in range(tiles):
            cols = slice(i * tile, (i + 1) * tile)
            s = enter[rs, cols]
            for t in range(frames):
                s = dec[t, rs, cols] * s + drv[t, rs, cols]
                states[t, :, cols] = s.astype(jnp.bfloat16)
        left_side = states[...].reshape(frames * part, width)
        square = None
        for i in range(tiles):
            cols = slice(i * tile, (i + 1) * tile)
            x = x_ref[:, rs, cols].reshape(frames * part, tile).astype(jnp.float32)
            m = x + nt(left_side, weight_rows(1, i))
            mixed[:, cols] = m
            square = m * m if i == 0 else square + m * m
        scaling = lax.rsqrt(jnp.sum(square, axis=1, keepdims=True) * (1.0 / width) + 1e-06)
        normed = (mixed[...] * scaling * gain_ref[...]).astype(jnp.bfloat16)
        by_frame = nt(normed, wb[...])
        values = by_frame[0:part]
        for t in range(1, frames):
            values = values + pltpu.roll(by_frame[t * part:(t + 1) * part], t * bits, axis=1)
        logits[rs, :] = values.astype(jnp.bfloat16)
        lane = lax.broadcasted_iota(jnp.int32, (part, LANES), 1)
        frame = (lane // bits).astype(jnp.float32)
        weight = jnp.where((len_b[rs, :] > frame) & (lane < packed), 1.0, 0.0)
        scaled = 4.0 * values
        size = jnp.abs(scaled)
        e = jnp.exp(-size)
        inverse = 1.0 / (1.0 + e)
        chance = jnp.where(scaled >= 0.0, inverse, e * inverse)
        entropy = jnp.log(1.0 + e) + size * e * inverse
        commit = jnp.square(jnp.abs(values) - 1.0)
        for row, value in enumerate((chance, entropy, commit, None)):
            kept = weight if value is None else value * weight
            sums[row:row + 1, :] += jnp.sum(kept, axis=0, keepdims=True)

    is_core1 = core == 1
    sibling_arrived(0)
    for k in range(CHUNKS):
        drives(k)
        if k >= 1:
            @pl.when(is_core1 & (chip == 0))
            def _():
                pass_chunk(k - 1, True, False)
        if k == 0:
            for item in range(1, early + 1):
                arrive(1, item)

    @pl.when(is_core1 & (chip == 0))
    def _():
        pass_chunk(CHUNKS - 1, True, False)

    @pl.when(is_core1 & (chip == 1) & (chip < chips - 1))
    def _():
        pass_half(0)
        pass_half(1)

    @pl.when(is_core1 & (chip > 1) & (chip < chips - 1))
    def _():
        pass_half(0)

    for item in range(early + 1, count):
        arrive(1, item)

    @pl.when(is_core1 & (chip > 1) & (chip < chips - 1))
    def _():
        pass_half(1)

    sibling_arrived(1)
    for k in range(CHUNKS):
        @pl.when(is_core1 & (chip == chips - 1))
        def _():
            pass_chunk(k, False, True)

        @pl.when(core == 0)
        def _():
            for j in range(k * per_chunk, (k + 1) * per_chunk):
                @pl.when(chip > 0)
                def _():
                    remote(ent.at[j], fwd_send.at[j], chain_recv.at[j], (me, sibling)).wait_recv()

                enter[j * piece:(j + 1) * piece, :] = ent[j].astype(jnp.float32)

        outputs(k)

    def share(buffer, own, stage, value, peer_of):
        buffer[own] = value
        for step in range(1, buffer.shape[0]):
            remote(
                buffer.at[own], sum_send.at[stage], sum_recv.at[stage], peer_of(step)
            ).start()

    def shared(buffer, stage):
        return remote(
            buffer.at[pl.ds(0, buffer.shape[0] - 1)], sum_send.at[stage], sum_recv.at[stage],
            (me, sibling),
        )

    def total_of(buffer, stage):
        shared(buffer, stage).wait_recv()
        total = buffer[0]
        for i in range(1, buffer.shape[0]):
            total = total + buffer[i]
        return total

    share(tmbuf, tm, 0, sums[...], lambda step: (me, (tm + step) % tm_count))
    dealt = nn(onehot[...], logits[...])
    sendbuf[...] = dealt.reshape(dp_count, 8, LANES)
    recvbuf[me, 0:GROUP] = sendbuf[me, 0:GROUP]

    def from_far(i):
        return n // 2 + (i // 2) * (1 - 2 * (i % 2)) - i % 2

    def deal(step):
        peer = (y + from_far(step // n)) % n * n + (z + from_far(step % n)) % n
        pltpu.make_async_remote_copy(
            src_ref=sendbuf.at[peer, pl.ds(0, GROUP)], dst_ref=recvbuf.at[me, pl.ds(0, GROUP)],
            send_sem=a2a_send, recv_sem=a2a_recv, device_id=(peer, tm), device_id_type=MESH,
        ).start()

    unrolled = 3 if (dp_count - 1) % 3 == 0 else 1

    def deal_some(i, carry):
        for j in range(unrolled):
            deal(i * unrolled + j)
        return carry

    lax.fori_loop(0, (dp_count - 1) // unrolled, deal_some, 0)

    share(zbuf, z, 1, total_of(tmbuf, 0), lambda step: (y * n + (z + step) % n, tm))

    for w in range(2):
        p1_all(w).wait_send()
        p2_all(w).wait_send()
        ours = wt.at[w, pl.ds(2 * core, 2)]
        remote(ours, sib_send.at[w], sib_recv.at[w], (me, sibling)).wait_send()
    remote(wt.at[0, mine], xs_send, xs_recv.at[0], (me, sibling)).wait_send()

    @pl.when(core == 0)
    def _():
        remote(reach, reach_send, reach_recv, (me, sibling)).wait_send()
        for k in range(CHUNKS):
            remote(
                local.at[pl.ds(k * part, part)], local_send.at[k], local_recv.at[k], (me, sibling)
            ).wait_send()

    @pl.when(is_core1)
    def _():
        for j in range(PIECES):
            @pl.when(chip < chips - 1)
            def _():
                remote(leave.at[j], chain_send.at[j], chain_recv.at[j], (me, sibling)).wait_send()

            @pl.when(chip > 0)
            def _():
                remote(ent.at[j], fwd_send.at[j], chain_recv.at[j], (me, sibling)).wait_send()

    arrived = remote(
        recvbuf.at[pl.ds(0, dp_count - 1), pl.ds(0, GROUP)], a2a_send, a2a_recv, (me, sibling)
    )
    share(ybuf, y, 2, total_of(zbuf, 1), lambda step: ((y + step) % n * n + z, tm))
    for stage, buffer in enumerate((tmbuf, zbuf)):
        shared(buffer, stage).wait_send()
    arrived.wait_send()
    arrived.wait_recv()
    turned = recvbuf[...].reshape(dp_count * 8, LANES).T.astype(jnp.bfloat16)
    placed = nn(turned, pick[...])
    for t in range(frames):
        staged[t] = placed[t * bits:(t + 1) * bits, :].astype(jnp.bfloat16)
    store = pltpu.make_async_copy(staged, codes_ref, store_sem)
    store.start()

    folded = total_of(ybuf, 2)
    folded = folded + pltpu.roll(folded, LANES - 3 * bits, axis=1)
    folded = (
        folded + pltpu.roll(folded, LANES - bits, axis=1)
        + pltpu.roll(folded, LANES - 2 * bits, axis=1)
    )
    is_bit = lax.broadcasted_iota(jnp.int32, (1, LANES), 1) < bits
    marginal = jnp.where(is_bit, folded[0:1] / folded[3:4], 0.5)
    terms = -marginal * jnp.log(marginal) - (1.0 - marginal) * jnp.log(1.0 - marginal)
    slots = 1.0 / float(rows * dp_count * frames * tm_count)
    shares = (folded[1:2] + 0.25 * folded[2:3]) * slots - terms
    penalty_ref[0, 0] = jnp.sum(jnp.where(is_bit, shares, 0.0))
    shared(ybuf, 2).wait_send()
    store.wait()


def shards(latents, lengths, plan, w_in, w_down, w_up, w_out, rate, gain, w_bits):
    rows, frames, width = latents.shape
    dp_count, tm_count = lax.axis_size("dp"), lax.axis_size("tm")
    n = math.isqrt(dp_count)
    bits = w_bits.shape[1]
    narrow_width = w_down.shape[1]
    part = rows // CHUNKS
    block = width // dp_count
    bf16, f32 = jnp.bfloat16, jnp.float32
    dma = pltpu.SemaphoreType.DMA
    codes, penalty = pl.pallas_call(
        functools.partial(kernel, dp_count, tm_count),
        out_shape=(
            jax.ShapeDtypeStruct((frames, bits, rows), bf16),
            jax.ShapeDtypeStruct((1, 1), f32),
        ),
        in_specs=[pl.BlockSpec(memory_space=pl.ANY)] * 10,
        out_specs=(pl.BlockSpec(memory_space=pl.ANY), pl.BlockSpec(memory_space=pltpu.SMEM)),
        scratch_shapes=[
            pltpu.VMEM((1, rows), jnp.int32),
            pltpu.VMEM((1, rows), jnp.int32),
            pltpu.VMEM((block, width), bf16),
            pltpu.VMEM((narrow_width, width), bf16),
            pltpu.VMEM((narrow_width, width), bf16),
            pltpu.VMEM((block, width), bf16),
            pltpu.VMEM((1, width), f32),
            pltpu.VMEM((1, width), f32),
            pltpu.VMEM((bits, width), bf16),
            dma((9,)),
            pltpu.VMEM((frames, rows, width), bf16),
            pltpu.VMEM((2, 4, n, n, block, width // 4), bf16),
            pltpu.VMEM((frames, rows, narrow_width), bf16),
            pltpu.VMEM((frames, rows, width), f32),
            pltpu.VMEM((frames, rows, width), f32),
            pltpu.VMEM((rows, width), f32),
            pltpu.VMEM((rows, width), f32),
            pltpu.VMEM((rows, width), f32),
            pltpu.VMEM((rows, width), f32),
            pltpu.VMEM((PIECES, rows // PIECES, width), bf16),
            pltpu.VMEM((PIECES, rows // PIECES, width), bf16),
            pltpu.VMEM((rows, width), f32),
            pltpu.VMEM((frames, part, width), bf16),
            pltpu.VMEM((frames * part, width), f32),
            pltpu.VMEM((LANES, width), bf16),
            pltpu.VMEM((dp_count * 8, rows), bf16),
            pltpu.VMEM((dp_count * 8, rows), bf16),
            pltpu.VMEM((rows, LANES), f32),
            pltpu.VMEM((rows, LANES), bf16),
            pltpu.VMEM((8, LANES), f32),
            pltpu.VMEM((dp_count, 8, LANES), f32),
            pltpu.VMEM((dp_count, 8, LANES), f32),
            pltpu.VMEM((tm_count, 8, LANES), f32),
            pltpu.VMEM((n, 8, LANES), f32),
            pltpu.VMEM((n, 8, LANES), f32),
            pltpu.VMEM((frames, bits, rows), bf16),
            dma,
            dma((2,)), dma((2,)), dma((2,)), dma((2, n)),
            dma, dma((n + 1,)), dma((2,)), dma((2,)),
            dma, dma, dma((CHUNKS,)), dma((CHUNKS,)),
            dma((PIECES,)), dma((PIECES,)), dma((PIECES,)),
            dma, dma, dma((3,)), dma((3,)), dma,
        ],
        compiler_params=pltpu.CompilerParams(
            collective_id=0, has_side_effects=True, vmem_limit_bytes=56 * 1024 * 1024
        ),
    )(
        jnp.transpose(latents, (1, 0, 2)), lengths.reshape(1, rows), plan.reshape(1, rows),
        w_in.T, w_down.T, w_up, w_out.T, rate.reshape(1, width), gain.reshape(1, width), w_bits.T,
    )
    return jnp.transpose(codes, (1, 0, 2)), penalty[0, 0]


def solution(mesh):
    return jax.shard_map(
        shards,
        mesh=mesh,
        in_specs=(
            P("dp", "tm", None),
            P("dp"),
            P("dp"),
            P(None, "dp"),
            P(),
            P(),
            P(None, "dp"),
            P(),
            P(),
            P(),
        ),
        out_specs=(P(None, "tm", "dp"), P()),
        check_vma=False,
    )
```

```python
import functools
import math

import jax
import jax.numpy as jnp
from jax import lax
from jax.experimental import pallas as pl
from jax.experimental.pallas import tpu as pltpu
from jax.sharding import PartitionSpec as P

MESH = pl.DeviceIdType.MESH
GROUP = 4
LANES = 128
CHUNKS = 4
PIECES = 16
LOG2E = math.log2(math.e)


def nt(a, b):
    return lax.dot_general(a, b, (((1,), (1,)), ((), ())), preferred_element_type=jnp.float32)


def nn(a, b):
    return jnp.dot(a, b, preferred_element_type=jnp.float32)


def kernel(
    dp_count, tm_count, x_hbm, *refs,
):
    smalls, refs = refs[:9], refs[9:]
    codes_ref, penalty_ref, *refs = refs
    lengths_ref, plan_ref, win_ref, wdown_ref, wup_ref, wout_ref, rate_ref, gain_ref, wbits_ref = refs[:9]
    small_sem, *refs = refs[9:]
    (
        x_ref, wt, narrow, dec, drv, reach, local, reach0, local0, ent, leave, enter, states, mixed, wb,
        onehot, pick, len_b, logits, sums, sendbuf, recvbuf, tmbuf, dpbuf,
        x_sem, p1_send, p1_recv, p2_send, p2_recv, xs_send, xs_recv, sib_send, sib_recv,
        reach_send, reach_recv, local_send, local_recv, chain_send, chain_recv, fwd_send,
        a2a_send, a2a_recv, tm_send, tm_recv, dp_send, dp_recv,
    ) = refs
    frames, rows, width = x_ref.shape
    n = math.isqrt(dp_count)
    quarter = width // 4
    part = rows // CHUNKS
    piece = rows // PIECES
    per_chunk = PIECES // CHUNKS
    tile = min(256, width)
    tiles = width // tile
    bits = wbits_ref.shape[0]
    packed = bits * frames
    chips = tm_count // 2
    me = lax.axis_index("dp")
    tm = lax.axis_index("tm")
    y, z = me // n, me % n
    chip, core = tm // 2, tm % 2
    odd = chip % 2
    major = y * (1 - core) + z * core
    minor = z * (1 - core) + y * core
    mine = 2 * core + odd
    other = 2 * core + 1 - odd
    sibling = tm + 1 - 2 * core
    next_chip = ((chip + 1) % chips) * 2 + core
    last_chip = ((chip + chips - 1) % chips) * 2 + core

    def dp_of(major_id, minor_id):
        return (major_id * n + minor_id) * (1 - core) + (minor_id * n + major_id) * core

    def on_core(make):
        pl.when(core == 0)(lambda: make(0))
        pl.when(core == 1)(lambda: make(1))

    near = n // 4
    items = [(0, 0, n)]
    if n == 2:
        items += [(1, 0, n)]
    else:
        items += [(o, 0, n) for step in range(1, n // 2) for o in (-step, step)]
        items += [(n // 2, 0, n // 2), (n // 2, n // 2, n // 2)]
    early = 2 * near if n > 2 else 1

    x_copy = pltpu.make_async_copy(x_hbm, x_ref, x_sem)
    barrier = pltpu.get_barrier_semaphore()

    def greet(dp_id, tm_id):
        pl.semaphore_signal(barrier, inc=1, device_id=(dp_id, tm_id), device_id_type=MESH)

    nearest = [o for step in range(1, near + 1) for o in (step, -step)] or [1]
    for offset in nearest:
        greet(dp_of(major, (minor + n + offset) % n), tm)
    for offset in nearest:
        greet(dp_of((major + n + offset) % n, minor), tm)
    for step in range(1, tm_count):
        greet(me, (tm + step) % tm_count)

    small_copies = [
        pltpu.make_async_copy(source, target, small_sem.at[i])
        for i, (source, target) in enumerate(zip(smalls, (
            lengths_ref, plan_ref, win_ref, wdown_ref, wup_ref, wout_ref, rate_ref, gain_ref, wbits_ref
        )))
    ]
    for i in (2, 5, 3, 4, 6, 0, 1, 7, 8):
        small_copies[i].start()
    x_copy.start()
    small_copies[2].wait()
    small_copies[5].wait()

    wt[0, mine, y, z] = win_ref[:, pl.ds(pl.multiple_of(mine * quarter, quarter), quarter)]
    for i in range(2):
        start = pl.multiple_of((2 * core + i) * quarter, quarter)
        wt[1, 2 * core + i, y, z] = wout_ref[:, pl.ds(start, quarter)]

    @pl.when(chip == 0)
    def _():
        ent[...] = jnp.zeros_like(ent)

    recvbuf[...] = jnp.zeros_like(recvbuf)
    dpbuf[...] = jnp.zeros_like(dpbuf)
    pl.semaphore_wait(barrier, 2 * len(nearest) + (tm_count - 1))

    def remote(ref, send, recv, device):
        return pltpu.make_async_remote_copy(
            src_ref=ref, dst_ref=ref, send_sem=send, recv_sem=recv,
            device_id=device, device_id_type=MESH,
        )

    firsts, counts = (mine, 2 * core), (1, 2)

    def group(w, c, major_id, first=None, low=0, count=n):
        quarters = pl.ds(firsts[w] if first is None else first, counts[w])
        if c == 0:
            return wt.at[w, quarters, major_id, pl.ds(low, count)]
        return wt.at[w, quarters, pl.ds(low, count), major_id]

    def at(offset):
        return (major + n + offset) % n

    def held(w, c, item, first=None):
        offset, low, count = items[item]
        return group(w, c, at(offset), first, low, count)

    def quarters_of(w):
        return pl.ds(firsts[w], counts[w])

    def block_of(w, offset):
        there = (minor + n + offset) % n
        return wt.at[
            w, quarters_of(w), major * (1 - core) + there * core,
            there * (1 - core) + major * core,
        ]

    def send_block(w, offset, stage, toward):
        remote(
            block_of(w, offset), p1_send.at[w], p1_recv.at[w, stage],
            (dp_of(major, (minor + n + toward) % n), tm),
        ).start()

    def p1_some(w, stage, count):
        some = wt.at[w, quarters_of(w), 0, pl.ds(0, count)]
        return remote(some, p1_send.at[w], p1_recv.at[w, stage], (me, sibling))

    def p1_near(w):
        for offset in nearest:
            send_block(w, 0, 0, offset)

    def p1_far(w):
        p1_some(w, 0, len(nearest)).wait_recv()
        if n > 2:
            for step in range(near + 1, n // 2 + 1):
                send_block(w, near - step, 1, near)
                if step < n // 2:
                    send_block(w, step - near, 1, -near)

    def p2_all(w):
        some = wt.at[w, quarters_of(w), pl.ds(0, n - 1)]
        return remote(some, p2_send.at[w], p2_recv.at[w, 0], (me, sibling))

    def send_group(w, piece_ref, item, toward):
        remote(
            piece_ref, p2_send.at[w], p2_recv.at[w, item - 1], (dp_of(at(toward), minor), tm)
        ).start()

    def near_sends(w):
        if n > 2:
            p1_some(w, 1, n - 1 - len(nearest)).wait_recv()

        def make(c):
            for item in range(1, early + 1):
                send_group(w, group(w, c, major), item, -items[item][0])
            forward(w, c, 0)
        on_core(make)

    def far_sends(w, c, item):
        offset = items[item][0]
        if n == 2 or item > early:
            return
        side = 1 if offset > 0 else -1
        if abs(offset) + near < n // 2:
            send_group(w, held(w, c, item), items.index((offset + side * near, 0, n)), -side * near)
        else:
            low = 0 if side < 0 else n // 2
            target = items.index((n // 2, low, n // 2))
            send_group(w, group(w, c, at(offset), None, low, n // 2), target, -side * near)

    def forward(w, c, item):
        if w == 0:
            target = next_chip if item % 2 == 0 and item < n - 1 else last_chip
            remote(held(w, c, item), xs_send, xs_recv.at[item], (me, target)).start()
        remote(held(w, c, item), sib_send.at[w], sib_recv.at[w], (me, sibling)).start()

    def arrive(w, item):
        def make(c):
            remote(
                held(w, c, item), p2_send.at[w], p2_recv.at[w, item - 1], (me, sibling)
            ).wait_recv()
            far_sends(w, c, item)
            forward(w, c, item)
        on_core(make)

    def x_arrive(item):
        def make(c):
            theirs = held(0, c, item, other)
            remote(theirs, xs_send, xs_recv.at[item], (me, sibling)).wait_recv()
            remote(theirs, sib_send.at[0], sib_recv.at[0], (me, sibling)).start()
        on_core(make)

    def sibling_arrived(w):
        theirs = wt.at[w, pl.ds(2 * (1 - core), 2)]
        remote(theirs, sib_send.at[w], sib_recv.at[w], (me, sibling)).wait_recv()

    def small_things():
        for i in (0, 1, 7, 8):
            small_copies[i].wait()
        first = tm * frames
        lengths = jnp.broadcast_to(lengths_ref[...].astype(jnp.float32), (LANES, rows))
        len_b[...] = lengths.T - first.astype(jnp.float32)
        spread = dp_count * 8
        slot = lax.broadcasted_iota(jnp.int32, (rows, spread), 1)
        source = lax.broadcasted_iota(jnp.int32, (rows, spread), 0)
        kept = slot % 8 < GROUP
        expand = jnp.where(kept & ((slot // 8) * GROUP + slot % 8 == source), 1.0, 0.0)
        expand = expand.astype(jnp.bfloat16)
        pick[...] = expand.T
        plan_rows = jnp.broadcast_to(plan_ref[...].astype(jnp.float32), (8, rows))
        wanted = nn(plan_rows.astype(jnp.bfloat16), expand)[0:1]
        chosen = jnp.where(kept & (wanted == source.astype(jnp.float32)), 1.0, 0.0)
        onehot[...] = chosen.T.astype(jnp.bfloat16)
        place = lax.broadcasted_iota(jnp.int32, (LANES, bits), 0)
        bit = lax.broadcasted_iota(jnp.int32, (LANES, bits), 1)
        chooser = jnp.where(place == bit, 1.0, 0.0).astype(jnp.bfloat16)
        wb[...] = nn(chooser, wbits_ref[...]).astype(jnp.bfloat16)
        sums[...] = jnp.zeros_like(sums)

    def narrowing():
        for i in (3, 4, 6):
            small_copies[i].wait()
        x_copy.wait()
        for t in range(frames):
            narrow[t] = nt(x_ref[t], wdown_ref[...]).astype(jnp.bfloat16)

    def decays(t):
        for i in range(tiles):
            cols = slice(i * tile, (i + 1) * tile)
            u = nn(narrow[t], wup_ref[:, cols]) * LOG2E
            soft = jnp.maximum(u, 0.0) + jnp.log2(1.0 + jnp.exp2(-jnp.abs(u)))
            d = jnp.exp2(-rate_ref[:, cols] * soft)
            dec[t, :, cols] = d
            reach[:, cols] = d if t == 0 else reach[:, cols] * d

    def decay_frames(low, high):
        for t in range(low, min(high, frames)):
            decays(t)

    count = len(items)
    p1_near(0)
    p1_far(0)
    narrowing()
    decay_frames(0, 1)
    near_sends(0)
    p1_near(1)
    decay_frames(1, 3)
    for item in range(1, early + 1):
        arrive(0, item)
    p1_far(1)
    near_sends(1)
    decay_frames(3, 4)
    x_done = 0
    for item in range(early + 1, count):
        x_arrive(x_done)
        x_done += 1
        arrive(0, item)
    decay_frames(4, frames)

    @pl.when(core == 0)
    def _():
        pltpu.make_async_remote_copy(
            src_ref=reach, dst_ref=reach0, send_sem=reach_send, recv_sem=reach_recv,
            device_id=(me, sibling), device_id_type=MESH,
        ).start()

    small_things()
    while x_done < count:
        x_arrive(x_done)
        x_done += 1

    def weight_rows(w, i):
        per = n // tiles
        all_quarters = [wt[w, q, i * per:(i + 1) * per].reshape(tile, quarter) for q in range(4)]
        return jnp.concatenate(all_quarters, axis=1)

    def valid_of(k, t):
        rs = slice(k * part, (k + 1) * part)
        return jnp.where(len_b[rs, :] > float(t), 1.0, 0.0)

    def drives(k):
        rs = slice(k * part, (k + 1) * part)
        left_side = x_ref[:, rs, :].reshape(frames * part, width)
        for i in range(tiles):
            cols = slice(i * tile, (i + 1) * tile)
            pushed = nt(left_side, weight_rows(0, i)).reshape(frames, part, tile)
            running = None
            for t in range(frames):
                mask = jnp.concatenate([valid_of(k, t)] * max(1, tile // LANES), axis=1)[:, :tile]
                now = pushed[t] * mask
                drv[t, rs, cols] = now
                running = now if t == 0 else dec[t, rs, cols] * running + now
            local[rs, cols] = running

        @pl.when(core == 0)
        def _():
            pltpu.make_async_remote_copy(
                src_ref=local.at[pl.ds(k * part, part)], dst_ref=local0.at[pl.ds(k * part, part)],
                send_sem=local_send.at[k], recv_sem=local_recv.at[k],
                device_id=(me, sibling), device_id_type=MESH,
            ).start()

    def local_wait(k):
        remote(
            local0.at[pl.ds(k * part, part)], local_send.at[k], local_recv.at[k], (me, sibling)
        ).wait_recv()

    def reach_wait():
        remote(reach0, reach_send, reach_recv, (me, sibling)).wait_recv()

    def pass_on(j, sends=True, receives=True):
        rs = pl.ds(pl.multiple_of(j * piece, piece), piece)
        if receives:
            remote(ent.at[j], chain_send.at[j], chain_recv.at[j], (me, sibling)).wait_recv()
            remote(ent.at[j], fwd_send.at[j], chain_recv.at[j], (me, sibling)).start()
            between = reach0[rs, :] * ent[j].astype(jnp.float32) + local0[rs, :]
        else:
            between = local0[rs, :]
        enter[rs, :] = between
        if sends:
            leave[j] = (reach[rs, :] * between + local[rs, :]).astype(jnp.bfloat16)
            pltpu.make_async_remote_copy(
                src_ref=leave.at[j], dst_ref=ent.at[j],
                send_sem=chain_send.at[j], recv_sem=chain_recv.at[j],
                device_id=(me, next_chip), device_id_type=MESH,
            ).start()

    def pass_chunk(k, sends, receives):
        if k == 0:
            reach_wait()
        local_wait(k)
        for j in range(k * per_chunk, (k + 1) * per_chunk):
            pass_on(j, sends, receives)

    def pass_half(h):
        if h == 0:
            reach_wait()
        for k in range(h * CHUNKS // 2, (h + 1) * CHUNKS // 2):
            local_wait(k)

        def step(j, carry):
            pass_on(j)
            return carry

        lax.fori_loop(h * PIECES // 2, (h + 1) * PIECES // 2, step, 0)

    def outputs(k):
        rs = slice(k * part, (k + 1) * part)
        for i in range(tiles):
            cols = slice(i * tile, (i + 1) * tile)
            s = enter[rs, cols]
            for t in range(frames):
                s = dec[t, rs, cols] * s + drv[t, rs, cols]
                states[t, :, cols] = s.astype(jnp.bfloat16)
        left_side = states[...].reshape(frames * part, width)
        square = None
        for i in range(tiles):
            cols = slice(i * tile, (i + 1) * tile)
            x = x_ref[:, rs, cols].reshape(frames * part, tile).astype(jnp.float32)
            m = x + nt(left_side, weight_rows(1, i))
            mixed[:, cols] = m
            square = m * m if i == 0 else square + m * m
        scaling = lax.rsqrt(jnp.sum(square, axis=1, keepdims=True) * (1.0 / width) + 1e-06)
        normed = (mixed[...] * scaling * gain_ref[...]).astype(jnp.bfloat16)
        by_frame = nt(normed, wb[...])
        values = by_frame[0:part]
        for t in range(1, frames):
            values = values + pltpu.roll(by_frame[t * part:(t + 1) * part], t * bits, axis=1)
        logits[rs, :] = values.astype(jnp.bfloat16)
        lane = lax.broadcasted_iota(jnp.int32, (part, LANES), 1)
        frame = (lane // bits).astype(jnp.float32)
        weight = jnp.where((len_b[rs, :] > frame) & (lane < packed), 1.0, 0.0)
        scaled = 4.0 * values
        size = jnp.abs(scaled)
        e = jnp.exp(-size)
        inverse = 1.0 / (1.0 + e)
        chance = jnp.where(scaled >= 0.0, inverse, e * inverse)
        entropy = jnp.log(1.0 + e) + size * e * inverse
        commit = jnp.square(jnp.abs(values) - 1.0)
        for row, value in enumerate((chance, entropy, commit, None)):
            kept = weight if value is None else value * weight
            sums[row:row + 1, :] += jnp.sum(kept, axis=0, keepdims=True)

    is_core1 = core == 1
    sibling_arrived(0)
    for k in range(CHUNKS):
        drives(k)
        if k >= 1:
            @pl.when(is_core1 & (chip == 0))
            def _():
                pass_chunk(k - 1, True, False)
        if k == 0:
            for item in range(1, early + 1):
                arrive(1, item)

    @pl.when(is_core1 & (chip == 0))
    def _():
        pass_chunk(CHUNKS - 1, True, False)

    @pl.when(is_core1 & (chip == 1) & (chip < chips - 1))
    def _():
        pass_half(0)
        pass_half(1)

    @pl.when(is_core1 & (chip > 1) & (chip < chips - 1))
    def _():
        pass_half(0)

    for item in range(early + 1, count):
        arrive(1, item)

    @pl.when(is_core1 & (chip > 1) & (chip < chips - 1))
    def _():
        pass_half(1)

    sibling_arrived(1)
    for k in range(CHUNKS):
        @pl.when(is_core1 & (chip == chips - 1))
        def _():
            pass_chunk(k, False, True)

        @pl.when(core == 0)
        def _():
            for j in range(k * per_chunk, (k + 1) * per_chunk):
                @pl.when(chip > 0)
                def _():
                    remote(ent.at[j], fwd_send.at[j], chain_recv.at[j], (me, sibling)).wait_recv()

                enter[j * piece:(j + 1) * piece, :] = ent[j].astype(jnp.float32)

        outputs(k)

    folded = sums[...]
    folded = folded + pltpu.roll(folded, LANES - 3 * bits, axis=1)
    folded = (
        folded + pltpu.roll(folded, LANES - bits, axis=1)
        + pltpu.roll(folded, LANES - 2 * bits, axis=1)
    )
    lane1 = lax.broadcasted_iota(jnp.int32, (1, LANES), 1)
    is_bit = lane1 < bits
    one_row = jnp.zeros((1, LANES), jnp.float32)
    for row in range(4):
        kept = jnp.where(is_bit, folded[row:row + 1], 0.0)
        one_row = one_row + (pltpu.roll(kept, row * bits, axis=1) if row else kept)
    tmbuf[tm, 0:1] = one_row
    for step in range(1, tm_count):
        remote(
            tmbuf.at[tm, pl.ds(0, 1)], tm_send, tm_recv, (me, (tm + step) % tm_count)
        ).start()

    dealt = nn(onehot[...], logits[...])
    sendbuf[...] = dealt.reshape(dp_count, 8, LANES)
    recvbuf[me, 0:GROUP] = sendbuf[me, 0:GROUP]

    def from_far(i):
        return n // 2 + (i // 2) * (1 - 2 * (i % 2)) - i % 2

    def peer_of(step):
        return (y + from_far(step // n)) % n * n + (z + from_far(step % n)) % n

    def deal(step):
        peer = peer_of(step)
        pltpu.make_async_remote_copy(
            src_ref=sendbuf.at[peer, pl.ds(0, GROUP)], dst_ref=recvbuf.at[me, pl.ds(0, GROUP)],
            send_sem=a2a_send, recv_sem=a2a_recv, device_id=(peer, tm), device_id_type=MESH,
        ).start()

    unrolled = 3 if (dp_count - 1) % 3 == 0 else 1

    def for_peers(send):
        def some(i, carry):
            for j in range(unrolled):
                send(i * unrolled + j)
            return carry

        lax.fori_loop(0, (dp_count - 1) // unrolled, some, 0)

    for_peers(deal)
    tm_all = remote(tmbuf.at[pl.ds(0, tm_count - 1), pl.ds(0, 1)], tm_send, tm_recv, (me, sibling))
    tm_all.wait_recv()
    total = tmbuf[0, 0:1]
    for i in range(1, tm_count):
        total = total + tmbuf[i, 0:1]
    dpbuf[me, 0:1] = total

    def spread(step):
        remote(
            dpbuf.at[me, pl.ds(0, 1)], dp_send, dp_recv, (peer_of(step), tm)
        ).start()

    for_peers(spread)
    dp_all = remote(dpbuf.at[pl.ds(0, dp_count - 1), pl.ds(0, 1)], dp_send, dp_recv, (me, sibling))

    for w in range(2):
        p1_some(w, 0, n - 1).wait_send()
        p2_all(w).wait_send()
        ours = wt.at[w, pl.ds(2 * core, 2)]
        remote(ours, sib_send.at[w], sib_recv.at[w], (me, sibling)).wait_send()
    remote(wt.at[0, mine], xs_send, xs_recv.at[0], (me, sibling)).wait_send()

    @pl.when(core == 0)
    def _():
        remote(reach, reach_send, reach_recv, (me, sibling)).wait_send()
        for k in range(CHUNKS):
            remote(
                local.at[pl.ds(k * part, part)], local_send.at[k], local_recv.at[k], (me, sibling)
            ).wait_send()

    @pl.when(is_core1)
    def _():
        for j in range(PIECES):
            @pl.when(chip < chips - 1)
            def _():
                remote(leave.at[j], chain_send.at[j], chain_recv.at[j], (me, sibling)).wait_send()

            @pl.when(chip > 0)
            def _():
                remote(ent.at[j], fwd_send.at[j], chain_recv.at[j], (me, sibling)).wait_send()

    arrived = remote(
        recvbuf.at[pl.ds(0, dp_count - 1), pl.ds(0, GROUP)], a2a_send, a2a_recv, (me, sibling)
    )
    tm_all.wait_send()
    arrived.wait_send()
    arrived.wait_recv()
    turned = recvbuf[...].reshape(dp_count * 8, LANES).T.astype(jnp.bfloat16)
    placed = nn(turned, pick[...])
    for t in range(frames):
        codes_ref[t] = placed[t * bits:(t + 1) * bits, :].astype(jnp.bfloat16)

    dp_all.wait_recv()
    everything = jnp.sum(dpbuf[...], axis=0)[0:1]
    parts = [everything] + [pltpu.roll(everything, LANES - row * bits, axis=1) for row in (1, 2, 3)]
    marginal = jnp.where(is_bit, parts[0] / parts[3], 0.5)
    terms = -marginal * jnp.log(marginal) - (1.0 - marginal) * jnp.log(1.0 - marginal)
    slots = 1.0 / float(rows * dp_count * frames * tm_count)
    shares = (parts[1] + 0.25 * parts[2]) * slots - terms
    penalty_ref[0, 0] = jnp.sum(jnp.where(is_bit, shares, 0.0))
    dp_all.wait_send()


def shards(latents, lengths, plan, w_in, w_down, w_up, w_out, rate, gain, w_bits):
    rows, frames, width = latents.shape
    dp_count, tm_count = lax.axis_size("dp"), lax.axis_size("tm")
    n = math.isqrt(dp_count)
    bits = w_bits.shape[1]
    narrow_width = w_down.shape[1]
    part = rows // CHUNKS
    block = width // dp_count
    bf16, f32 = jnp.bfloat16, jnp.float32
    dma = pltpu.SemaphoreType.DMA
    codes, penalty = pl.pallas_call(
        functools.partial(kernel, dp_count, tm_count),
        out_shape=(
            pltpu.VMEM((frames, bits, rows), bf16),
            jax.ShapeDtypeStruct((1, 1), f32),
        ),
        in_specs=[pl.BlockSpec(memory_space=pl.ANY)] * 10,
        out_specs=(pl.BlockSpec(memory_space=pltpu.VMEM), pl.BlockSpec(memory_space=pltpu.SMEM)),
        scratch_shapes=[
            pltpu.VMEM((1, rows), jnp.int32),
            pltpu.VMEM((1, rows), jnp.int32),
            pltpu.VMEM((block, width), bf16),
            pltpu.VMEM((narrow_width, width), bf16),
            pltpu.VMEM((narrow_width, width), bf16),
            pltpu.VMEM((block, width), bf16),
            pltpu.VMEM((1, width), f32),
            pltpu.VMEM((1, width), f32),
            pltpu.VMEM((bits, width), bf16),
            dma((9,)),
            pltpu.VMEM((frames, rows, width), bf16),
            pltpu.VMEM((2, 4, n, n, block, width // 4), bf16),
            pltpu.VMEM((frames, rows, narrow_width), bf16),
            pltpu.VMEM((frames, rows, width), f32),
            pltpu.VMEM((frames, rows, width), f32),
            pltpu.VMEM((rows, width), f32),
            pltpu.VMEM((rows, width), f32),
            pltpu.VMEM((rows, width), f32),
            pltpu.VMEM((rows, width), f32),
            pltpu.VMEM((PIECES, rows // PIECES, width), bf16),
            pltpu.VMEM((PIECES, rows // PIECES, width), bf16),
            pltpu.VMEM((rows, width), f32),
            pltpu.VMEM((frames, part, width), bf16),
            pltpu.VMEM((frames * part, width), f32),
            pltpu.VMEM((LANES, width), bf16),
            pltpu.VMEM((dp_count * 8, rows), bf16),
            pltpu.VMEM((dp_count * 8, rows), bf16),
            pltpu.VMEM((rows, LANES), f32),
            pltpu.VMEM((rows, LANES), bf16),
            pltpu.VMEM((8, LANES), f32),
            pltpu.VMEM((dp_count, 8, LANES), f32),
            pltpu.VMEM((dp_count, 8, LANES), f32),
            pltpu.VMEM((tm_count, 8, LANES), f32),
            pltpu.VMEM((dp_count, 8, LANES), f32),
            dma,
            dma((2,)), dma((2, 2)), dma((2,)), dma((2, n)),
            dma, dma((n + 1,)), dma((2,)), dma((2,)),
            dma, dma, dma((CHUNKS,)), dma((CHUNKS,)),
            dma((PIECES,)), dma((PIECES,)), dma((PIECES,)),
            dma, dma, dma, dma, dma, dma,
        ],
        compiler_params=pltpu.CompilerParams(
            collective_id=0, has_side_effects=True, vmem_limit_bytes=56 * 1024 * 1024
        ),
    )(
        jnp.transpose(latents, (1, 0, 2)), lengths.reshape(1, rows), plan.reshape(1, rows),
        w_in.T, w_down.T, w_up, w_out.T, rate.reshape(1, width), gain.reshape(1, width), w_bits.T,
    )
    return jnp.transpose(codes, (1, 0, 2)), penalty[0, 0]


def solution(mesh):
    return jax.shard_map(
        shards,
        mesh=mesh,
        in_specs=(
            P("dp", "tm", None),
            P("dp"),
            P("dp"),
            P(None, "dp"),
            P(),
            P(),
            P(None, "dp"),
            P(),
            P(),
            P(),
        ),
        out_specs=(P(None, "tm", "dp"), P()),
        check_vma=False,
    )
```

```python
import functools
import math

import jax
import jax.numpy as jnp
from jax import lax
from jax.experimental import pallas as pl
from jax.experimental.pallas import tpu as pltpu
from jax.sharding import PartitionSpec as P

MESH = pl.DeviceIdType.MESH
GROUP = 4
LANES = 128
ENDS = (2, 4, 6, 8)
CHUNKS = len(ENDS)
PIECES = 16
LOG2E = math.log2(math.e)


def nt(a, b):
    return lax.dot_general(a, b, (((1,), (1,)), ((), ())), preferred_element_type=jnp.float32)


def nn(a, b):
    return jnp.dot(a, b, preferred_element_type=jnp.float32)


def kernel(
    dp_count, tm_count, x_hbm, *refs,
):
    smalls, refs = refs[:9], refs[9:]
    codes_ref, penalty_ref, *refs = refs
    lengths_ref, plan_ref, win_ref, wdown_ref, wup_ref, wout_ref, rate_ref, gain_ref, wbits_ref = refs[:9]
    small_sem, *refs = refs[9:]
    (
        x_ref, wt, narrow, dec, drv, reach, local, reach0, local0, ent, leave, enter, states, mixed, wb,
        onehot, pick, len_b, logits, sums, sendbuf, recvbuf, tmbuf, zbuf, ybuf,
        x_sem, p1_send, p1_recv, p2_send, p2_recv, xs_send, xs_recv, sib_send, sib_recv,
        reach_send, reach_recv, local_send, local_recv, chain_send, chain_recv, fwd_send,
        a2a_send, a2a_recv, sum_send, sum_recv,
    ) = refs
    frames, rows, width = x_ref.shape
    n = math.isqrt(dp_count)
    quarter = width // 4
    piece = rows // PIECES
    ends = [end * rows // 8 for end in ENDS]
    starts = [0] + ends[:-1]
    parts_of = [end - start for start, end in zip(starts, ends)]
    tile = min(256, width)
    tiles = width // tile
    bits = wbits_ref.shape[0]
    packed = bits * frames
    chips = tm_count // 2
    me = lax.axis_index("dp")
    tm = lax.axis_index("tm")
    y, z = me // n, me % n
    chip, core = tm // 2, tm % 2
    odd = chip % 2
    major = y * (1 - core) + z * core
    minor = z * (1 - core) + y * core
    mine = 2 * core + odd
    other = 2 * core + 1 - odd
    sibling = tm + 1 - 2 * core
    next_chip = ((chip + 1) % chips) * 2 + core
    last_chip = ((chip + chips - 1) % chips) * 2 + core

    def dp_of(major_id, minor_id):
        return (major_id * n + minor_id) * (1 - core) + (minor_id * n + major_id) * core

    def on_core(make):
        pl.when(core == 0)(lambda: make(0))
        pl.when(core == 1)(lambda: make(1))

    near = n // 4
    items = [(0, 0, n)]
    if n == 2:
        items += [(1, 0, n)]
    else:
        items += [(o, 0, n) for step in range(1, n // 2) for o in (-step, step)]
        items += [(n // 2, 0, n // 2), (n // 2, n // 2, n // 2)]
    early = 2 * near if n > 2 else 1

    x_copy = pltpu.make_async_copy(x_hbm, x_ref, x_sem)
    barrier = pltpu.get_barrier_semaphore()

    def greet(dp_id, tm_id):
        pl.semaphore_signal(barrier, inc=1, device_id=(dp_id, tm_id), device_id_type=MESH)

    for step in range(1, n):
        greet(dp_of(major, (minor + step) % n), tm)
    for step in range(1, n):
        greet(dp_of((major + step) % n, minor), tm)
    for step in range(1, tm_count):
        greet(me, (tm + step) % tm_count)

    small_copies = [
        pltpu.make_async_copy(source, target, small_sem.at[i])
        for i, (source, target) in enumerate(zip(smalls, (
            lengths_ref, plan_ref, win_ref, wdown_ref, wup_ref, wout_ref, rate_ref, gain_ref, wbits_ref
        )))
    ]
    for i in (2, 5, 3, 4, 6, 0, 1, 7, 8):
        small_copies[i].start()
    x_copy.start()
    small_copies[2].wait()
    small_copies[5].wait()

    wt[0, mine, y, z] = win_ref[:, pl.ds(pl.multiple_of(mine * quarter, quarter), quarter)]
    for i in range(2):
        start = pl.multiple_of((2 * core + i) * quarter, quarter)
        wt[1, 2 * core + i, y, z] = wout_ref[:, pl.ds(start, quarter)]

    @pl.when(chip == 0)
    def _():
        ent[...] = jnp.zeros_like(ent)

    recvbuf[...] = jnp.zeros_like(recvbuf)
    pl.semaphore_wait(barrier, 2 * (n - 1) + (tm_count - 1))

    def remote(ref, send, recv, device):
        return pltpu.make_async_remote_copy(
            src_ref=ref, dst_ref=ref, send_sem=send, recv_sem=recv,
            device_id=device, device_id_type=MESH,
        )

    firsts, counts = (mine, 2 * core), (1, 2)

    def group(w, c, major_id, first=None, low=0, count=n):
        quarters = pl.ds(firsts[w] if first is None else first, counts[w])
        if c == 0:
            return wt.at[w, quarters, major_id, pl.ds(low, count)]
        return wt.at[w, quarters, pl.ds(low, count), major_id]

    def at(offset):
        return (major + n + offset) % n

    def held(w, c, item, first=None):
        offset, low, count = items[item]
        return group(w, c, at(offset), first, low, count)

    def quarters_of(w):
        return pl.ds(firsts[w], counts[w])

    def p1_start(w):
        for step in range(1, n):
            remote(
                wt.at[w, quarters_of(w), y, z], p1_send.at[w], p1_recv.at[w],
                (dp_of(major, (minor + step) % n), tm),
            ).start()

    def p1_all(w):
        some = wt.at[w, quarters_of(w), 0, pl.ds(0, n - 1)]
        return remote(some, p1_send.at[w], p1_recv.at[w], (me, sibling))

    def p2_all(w):
        some = wt.at[w, quarters_of(w), pl.ds(0, n - 1)]
        return remote(some, p2_send.at[w], p2_recv.at[w, 0], (me, sibling))

    def send_group(w, piece_ref, item, toward):
        remote(
            piece_ref, p2_send.at[w], p2_recv.at[w, item - 1], (dp_of(at(toward), minor), tm)
        ).start()

    def near_sends(w):
        p1_all(w).wait_recv()

        def make(c):
            for item in range(1, early + 1):
                send_group(w, group(w, c, major), item, -items[item][0])
            forward(w, c, 0)
        on_core(make)

    def far_sends(w, c, item):
        offset = items[item][0]
        if n == 2 or item > early:
            return
        side = 1 if offset > 0 else -1
        if abs(offset) + near < n // 2:
            send_group(w, held(w, c, item), items.index((offset + side * near, 0, n)), -side * near)
        else:
            low = 0 if side < 0 else n // 2
            target = items.index((n // 2, low, n // 2))
            send_group(w, group(w, c, at(offset), None, low, n // 2), target, -side * near)

    def forward(w, c, item):
        if w == 0:
            target = next_chip if item % 2 == 0 and item < n - 1 else last_chip
            remote(held(w, c, item), xs_send, xs_recv.at[item], (me, target)).start()
        remote(held(w, c, item), sib_send.at[w], sib_recv.at[w], (me, sibling)).start()

    def arrive(w, item):
        def make(c):
            remote(
                held(w, c, item), p2_send.at[w], p2_recv.at[w, item - 1], (me, sibling)
            ).wait_recv()
            far_sends(w, c, item)
            forward(w, c, item)
        on_core(make)

    def x_arrive(item):
        def make(c):
            theirs = held(0, c, item, other)
            remote(theirs, xs_send, xs_recv.at[item], (me, sibling)).wait_recv()
            remote(theirs, sib_send.at[0], sib_recv.at[0], (me, sibling)).start()
        on_core(make)

    def sibling_arrived(w):
        theirs = wt.at[w, pl.ds(2 * (1 - core), 2)]
        remote(theirs, sib_send.at[w], sib_recv.at[w], (me, sibling)).wait_recv()

    def small_things():
        for i in (0, 1, 7, 8):
            small_copies[i].wait()
        first = tm * frames
        lengths = jnp.broadcast_to(lengths_ref[...].astype(jnp.float32), (LANES, rows))
        len_b[...] = lengths.T - first.astype(jnp.float32)
        spread = dp_count * 8
        slot = lax.broadcasted_iota(jnp.int32, (rows, spread), 1)
        source = lax.broadcasted_iota(jnp.int32, (rows, spread), 0)
        kept = slot % 8 < GROUP
        expand = jnp.where(kept & ((slot // 8) * GROUP + slot % 8 == source), 1.0, 0.0)
        expand = expand.astype(jnp.bfloat16)
        pick[...] = expand.T
        plan_rows = jnp.broadcast_to(plan_ref[...].astype(jnp.float32), (8, rows))
        wanted = nn(plan_rows.astype(jnp.bfloat16), expand)[0:1]
        chosen = jnp.where(kept & (wanted == source.astype(jnp.float32)), 1.0, 0.0)
        onehot[...] = chosen.T.astype(jnp.bfloat16)
        place = lax.broadcasted_iota(jnp.int32, (LANES, bits), 0)
        bit = lax.broadcasted_iota(jnp.int32, (LANES, bits), 1)
        chooser = jnp.where(place == bit, 1.0, 0.0).astype(jnp.bfloat16)
        wb[...] = nn(chooser, wbits_ref[...]).astype(jnp.bfloat16)
        sums[...] = jnp.zeros_like(sums)

    def narrowing():
        for i in (3, 4, 6):
            small_copies[i].wait()
        x_copy.wait()
        for t in range(frames):
            narrow[t] = nt(x_ref[t], wdown_ref[...]).astype(jnp.bfloat16)

    def decays(t):
        for i in range(tiles):
            cols = slice(i * tile, (i + 1) * tile)
            u = nn(narrow[t], wup_ref[:, cols]) * LOG2E
            soft = jnp.maximum(u, 0.0) + jnp.log2(1.0 + jnp.exp2(-jnp.abs(u)))
            d = jnp.exp2(-rate_ref[:, cols] * soft)
            dec[t, :, cols] = d
            reach[:, cols] = d if t == 0 else reach[:, cols] * d

    def decay_frames(low, high):
        for t in range(low, min(high, frames)):
            decays(t)

    count = len(items)
    p1_start(0)
    narrowing()
    decay_frames(0, 1)
    near_sends(0)
    p1_start(1)
    decay_frames(1, 3)
    for item in range(1, early + 1):
        arrive(0, item)
    near_sends(1)
    decay_frames(3, 4)
    x_done = 0
    for item in range(early + 1, count):
        x_arrive(x_done)
        x_done += 1
        arrive(0, item)
    decay_frames(4, frames)

    @pl.when(core == 0)
    def _():
        pltpu.make_async_remote_copy(
            src_ref=reach, dst_ref=reach0, send_sem=reach_send, recv_sem=reach_recv,
            device_id=(me, sibling), device_id_type=MESH,
        ).start()

    small_things()
    while x_done < count:
        x_arrive(x_done)
        x_done += 1

    def weight_rows(w, i):
        per = n // tiles
        all_quarters = [wt[w, q, i * per:(i + 1) * per].reshape(tile, quarter) for q in range(4)]
        return jnp.concatenate(all_quarters, axis=1)

    def valid_of(k, t):
        rs = slice(starts[k], ends[k])
        return jnp.where(len_b[rs, :] > float(t), 1.0, 0.0)

    def drives(k):
        rs, part = slice(starts[k], ends[k]), parts_of[k]
        left_side = x_ref[:, rs, :].reshape(frames * part, width)
        for i in range(tiles):
            cols = slice(i * tile, (i + 1) * tile)
            pushed = nt(left_side, weight_rows(0, i)).reshape(frames, part, tile)
            running = None
            for t in range(frames):
                mask = jnp.concatenate([valid_of(k, t)] * max(1, tile // LANES), axis=1)[:, :tile]
                now = pushed[t] * mask
                drv[t, rs, cols] = now
                running = now if t == 0 else dec[t, rs, cols] * running + now
            local[rs, cols] = running

        @pl.when(core == 0)
        def _():
            pltpu.make_async_remote_copy(
                src_ref=local.at[pl.ds(starts[k], part)], dst_ref=local0.at[pl.ds(starts[k], part)],
                send_sem=local_send.at[k], recv_sem=local_recv.at[k],
                device_id=(me, sibling), device_id_type=MESH,
            ).start()

    def local_wait(k):
        rs = pl.ds(starts[k], parts_of[k])
        remote(local0.at[rs], local_send.at[k], local_recv.at[k], (me, sibling)).wait_recv()

    def reach_wait():
        remote(reach0, reach_send, reach_recv, (me, sibling)).wait_recv()

    def pass_on(j, sends=True, receives=True):
        rs = pl.ds(pl.multiple_of(j * piece, piece), piece)
        if receives:
            remote(ent.at[j], chain_send.at[j], chain_recv.at[j], (me, sibling)).wait_recv()
            remote(ent.at[j], fwd_send.at[j], chain_recv.at[j], (me, sibling)).start()
            between = reach0[rs, :] * ent[j].astype(jnp.float32) + local0[rs, :]
        else:
            between = local0[rs, :]
        enter[rs, :] = between
        if sends:
            leave[j] = (reach[rs, :] * between + local[rs, :]).astype(jnp.bfloat16)
            pltpu.make_async_remote_copy(
                src_ref=leave.at[j], dst_ref=ent.at[j],
                send_sem=chain_send.at[j], recv_sem=chain_recv.at[j],
                device_id=(me, next_chip), device_id_type=MESH,
            ).start()

    def pass_chunk(k, sends, receives):
        if k == 0:
            reach_wait()
        local_wait(k)
        for j in range(starts[k] // piece, ends[k] // piece):
            pass_on(j, sends, receives)

    def pass_half(h):
        if h == 0:
            reach_wait()
        for k in range(CHUNKS):
            if (starts[k] >= rows // 2) == (h == 1):
                local_wait(k)

        def step(j, carry):
            pass_on(j)
            return carry

        lax.fori_loop(h * PIECES // 2, (h + 1) * PIECES // 2, step, 0)

    def outputs(k):
        rs, part = slice(starts[k], ends[k]), parts_of[k]
        count = frames * part
        for i in range(tiles):
            cols = slice(i * tile, (i + 1) * tile)
            s = enter[rs, cols]
            for t in range(frames):
                s = dec[t, rs, cols] * s + drv[t, rs, cols]
                states[t, 0:part, cols] = s.astype(jnp.bfloat16)
        left_side = states[:, 0:part].reshape(count, width)
        square = None
        for i in range(tiles):
            cols = slice(i * tile, (i + 1) * tile)
            x = x_ref[:, rs, cols].reshape(count, tile).astype(jnp.float32)
            m = x + nt(left_side, weight_rows(1, i))
            mixed[0:count, cols] = m
            square = m * m if i == 0 else square + m * m
        scaling = lax.rsqrt(jnp.sum(square, axis=1, keepdims=True) * (1.0 / width) + 1e-06)
        normed = (mixed[0:count] * scaling * gain_ref[...]).astype(jnp.bfloat16)
        by_frame = nt(normed, wb[...])
        values = by_frame[0:part]
        for t in range(1, frames):
            values = values + pltpu.roll(by_frame[t * part:(t + 1) * part], t * bits, axis=1)
        logits[rs, :] = values.astype(jnp.bfloat16)
        lane = lax.broadcasted_iota(jnp.int32, (part, LANES), 1)
        frame = (lane // bits).astype(jnp.float32)
        weight = jnp.where((len_b[rs, :] > frame) & (lane < packed), 1.0, 0.0)
        scaled = 4.0 * values
        size = jnp.abs(scaled)
        e = jnp.exp(-size)
        inverse = 1.0 / (1.0 + e)
        chance = jnp.where(scaled >= 0.0, inverse, e * inverse)
        entropy = jnp.log(1.0 + e) + size * e * inverse
        commit = jnp.square(jnp.abs(values) - 1.0)
        for row, value in enumerate((chance, entropy, commit, None)):
            kept = weight if value is None else value * weight
            sums[row:row + 1, :] += jnp.sum(kept, axis=0, keepdims=True)

    is_core1 = core == 1
    sibling_arrived(0)
    for k in range(CHUNKS):
        drives(k)
        if k >= 1:
            @pl.when(is_core1 & (chip == 0))
            def _():
                pass_chunk(k - 1, True, False)
        if k == 0:
            for item in range(1, early + 1):
                arrive(1, item)

    @pl.when(is_core1 & (chip == 0))
    def _():
        pass_chunk(CHUNKS - 1, True, False)

    @pl.when(is_core1 & (chip == 1) & (chip < chips - 1))
    def _():
        pass_half(0)
        pass_half(1)

    @pl.when(is_core1 & (chip > 1) & (chip < chips - 1))
    def _():
        pass_half(0)

    for item in range(early + 1, count):
        arrive(1, item)

    @pl.when(is_core1 & (chip > 1) & (chip < chips - 1))
    def _():
        pass_half(1)

    sibling_arrived(1)
    for k in range(CHUNKS):
        @pl.when(is_core1 & (chip == chips - 1))
        def _():
            pass_chunk(k, False, True)

        @pl.when(core == 0)
        def _():
            for j in range(starts[k] // piece, ends[k] // piece):
                @pl.when(chip > 0)
                def _():
                    remote(ent.at[j], fwd_send.at[j], chain_recv.at[j], (me, sibling)).wait_recv()

                enter[j * piece:(j + 1) * piece, :] = ent[j].astype(jnp.float32)

        outputs(k)

    folded = sums[...]
    folded = folded + pltpu.roll(folded, LANES - 3 * bits, axis=1)
    folded = (
        folded + pltpu.roll(folded, LANES - bits, axis=1)
        + pltpu.roll(folded, LANES - 2 * bits, axis=1)
    )
    is_bit = lax.broadcasted_iota(jnp.int32, (1, LANES), 1) < bits
    one_row = jnp.zeros((1, LANES), jnp.float32)
    for row in range(4):
        kept = jnp.where(is_bit, folded[row:row + 1], 0.0)
        one_row = one_row + (pltpu.roll(kept, row * bits, axis=1) if row else kept)

    def share(buffer, own, stage, value, peer_of):
        buffer[own, 0:1] = value
        for step in range(1, buffer.shape[0]):
            remote(
                buffer.at[own, pl.ds(0, 1)], sum_send.at[stage], sum_recv.at[stage], peer_of(step)
            ).start()

    def shared(buffer, stage):
        return remote(
            buffer.at[pl.ds(0, buffer.shape[0] - 1), pl.ds(0, 1)], sum_send.at[stage], sum_recv.at[stage],
            (me, sibling),
        )

    def total_of(buffer, stage):
        shared(buffer, stage).wait_recv()
        total = buffer[0, 0:1]
        for i in range(1, buffer.shape[0]):
            total = total + buffer[i, 0:1]
        return total

    share(tmbuf, tm, 0, one_row, lambda step: (me, (tm + step) % tm_count))
    dealt = nn(onehot[...], logits[...])
    sendbuf[...] = dealt.reshape(dp_count, 8, LANES)
    recvbuf[me, 0:GROUP] = sendbuf[me, 0:GROUP]

    def from_far(i):
        return n // 2 + (i // 2) * (1 - 2 * (i % 2)) - i % 2

    def deal(step):
        peer = (y + from_far(step // n)) % n * n + (z + from_far(step % n)) % n
        pltpu.make_async_remote_copy(
            src_ref=sendbuf.at[peer, pl.ds(0, GROUP)], dst_ref=recvbuf.at[me, pl.ds(0, GROUP)],
            send_sem=a2a_send, recv_sem=a2a_recv, device_id=(peer, tm), device_id_type=MESH,
        ).start()

    unrolled = 3 if (dp_count - 1) % 3 == 0 else 1

    def deal_some(i, carry):
        for j in range(unrolled):
            deal(i * unrolled + j)
        return carry

    lax.fori_loop(0, (dp_count - 1) // unrolled, deal_some, 0)

    share(zbuf, z, 1, total_of(tmbuf, 0), lambda step: (y * n + (z + step) % n, tm))

    for w in range(2):
        p1_all(w).wait_send()
        p2_all(w).wait_send()
        ours = wt.at[w, pl.ds(2 * core, 2)]
        remote(ours, sib_send.at[w], sib_recv.at[w], (me, sibling)).wait_send()
    remote(wt.at[0, mine], xs_send, xs_recv.at[0], (me, sibling)).wait_send()

    @pl.when(core == 0)
    def _():
        remote(reach, reach_send, reach_recv, (me, sibling)).wait_send()
        for k in range(CHUNKS):
            rs = pl.ds(starts[k], parts_of[k])
            remote(local.at[rs], local_send.at[k], local_recv.at[k], (me, sibling)).wait_send()

    @pl.when(is_core1)
    def _():
        for j in range(PIECES):
            @pl.when(chip < chips - 1)
            def _():
                remote(leave.at[j], chain_send.at[j], chain_recv.at[j], (me, sibling)).wait_send()

            @pl.when(chip > 0)
            def _():
                remote(ent.at[j], fwd_send.at[j], chain_recv.at[j], (me, sibling)).wait_send()

    arrived = remote(
        recvbuf.at[pl.ds(0, dp_count - 1), pl.ds(0, GROUP)], a2a_send, a2a_recv, (me, sibling)
    )
    share(ybuf, y, 2, total_of(zbuf, 1), lambda step: ((y + step) % n * n + z, tm))
    for stage, buffer in enumerate((tmbuf, zbuf)):
        shared(buffer, stage).wait_send()
    arrived.wait_send()
    arrived.wait_recv()
    turned = recvbuf[...].reshape(dp_count * 8, LANES).T.astype(jnp.bfloat16)
    placed = nn(turned, pick[...])
    for t in range(frames):
        codes_ref[t] = placed[t * bits:(t + 1) * bits, :].astype(jnp.bfloat16)

    everything = total_of(ybuf, 2)
    parts = [everything] + [pltpu.roll(everything, LANES - row * bits, axis=1) for row in (1, 2, 3)]
    marginal = jnp.where(is_bit, parts[0] / parts[3], 0.5)
    terms = -marginal * jnp.log(marginal) - (1.0 - marginal) * jnp.log(1.0 - marginal)
    slots = 1.0 / float(rows * dp_count * frames * tm_count)
    shares = (parts[1] + 0.25 * parts[2]) * slots - terms
    penalty_ref[0, 0] = jnp.sum(jnp.where(is_bit, shares, 0.0))
    shared(ybuf, 2).wait_send()


def shards(latents, lengths, plan, w_in, w_down, w_up, w_out, rate, gain, w_bits):
    rows, frames, width = latents.shape
    dp_count, tm_count = lax.axis_size("dp"), lax.axis_size("tm")
    n = math.isqrt(dp_count)
    bits = w_bits.shape[1]
    narrow_width = w_down.shape[1]
    part = rows // 4
    block = width // dp_count
    bf16, f32 = jnp.bfloat16, jnp.float32
    dma = pltpu.SemaphoreType.DMA
    codes, penalty = pl.pallas_call(
        functools.partial(kernel, dp_count, tm_count),
        out_shape=(
            pltpu.VMEM((frames, bits, rows), bf16),
            jax.ShapeDtypeStruct((1, 1), f32),
        ),
        in_specs=[pl.BlockSpec(memory_space=pl.ANY)] * 10,
        out_specs=(pl.BlockSpec(memory_space=pltpu.VMEM), pl.BlockSpec(memory_space=pltpu.SMEM)),
        scratch_shapes=[
            pltpu.VMEM((1, rows), jnp.int32),
            pltpu.VMEM((1, rows), jnp.int32),
            pltpu.VMEM((block, width), bf16),
            pltpu.VMEM((narrow_width, width), bf16),
            pltpu.VMEM((narrow_width, width), bf16),
            pltpu.VMEM((block, width), bf16),
            pltpu.VMEM((1, width), f32),
            pltpu.VMEM((1, width), f32),
            pltpu.VMEM((bits, width), bf16),
            dma((9,)),
            pltpu.VMEM((frames, rows, width), bf16),
            pltpu.VMEM((2, 4, n, n, block, width // 4), bf16),
            pltpu.VMEM((frames, rows, narrow_width), bf16),
            pltpu.VMEM((frames, rows, width), f32),
            pltpu.VMEM((frames, rows, width), f32),
            pltpu.VMEM((rows, width), f32),
            pltpu.VMEM((rows, width), f32),
            pltpu.VMEM((rows, width), f32),
            pltpu.VMEM((rows, width), f32),
            pltpu.VMEM((PIECES, rows // PIECES, width), bf16),
            pltpu.VMEM((PIECES, rows // PIECES, width), bf16),
            pltpu.VMEM((rows, width), f32),
            pltpu.VMEM((frames, part, width), bf16),
            pltpu.VMEM((frames * part, width), f32),
            pltpu.VMEM((LANES, width), bf16),
            pltpu.VMEM((dp_count * 8, rows), bf16),
            pltpu.VMEM((dp_count * 8, rows), bf16),
            pltpu.VMEM((rows, LANES), f32),
            pltpu.VMEM((rows, LANES), bf16),
            pltpu.VMEM((8, LANES), f32),
            pltpu.VMEM((dp_count, 8, LANES), f32),
            pltpu.VMEM((dp_count, 8, LANES), f32),
            pltpu.VMEM((tm_count, 8, LANES), f32),
            pltpu.VMEM((n, 8, LANES), f32),
            pltpu.VMEM((n, 8, LANES), f32),
            dma,
            dma((2,)), dma((2,)), dma((2,)), dma((2, n)),
            dma, dma((n + 1,)), dma((2,)), dma((2,)),
            dma, dma, dma((CHUNKS,)), dma((CHUNKS,)),
            dma((PIECES,)), dma((PIECES,)), dma((PIECES,)),
            dma, dma, dma((3,)), dma((3,)),
        ],
        compiler_params=pltpu.CompilerParams(
            collective_id=0, has_side_effects=True, vmem_limit_bytes=56 * 1024 * 1024
        ),
    )(
        jnp.transpose(latents, (1, 0, 2)), lengths.reshape(1, rows), plan.reshape(1, rows),
        w_in.T, w_down.T, w_up, w_out.T, rate.reshape(1, width), gain.reshape(1, width), w_bits.T,
    )
    return jnp.transpose(codes, (1, 0, 2)), penalty[0, 0]


def solution(mesh):
    return jax.shard_map(
        shards,
        mesh=mesh,
        in_specs=(
            P("dp", "tm", None),
            P("dp"),
            P("dp"),
            P(None, "dp"),
            P(),
            P(),
            P(None, "dp"),
            P(),
            P(),
            P(),
        ),
        out_specs=(P(None, "tm", "dp"), P()),
        check_vma=False,
    )
```

```python
import functools
import math

import jax
import jax.numpy as jnp
from jax import lax
from jax.experimental import pallas as pl
from jax.experimental.pallas import tpu as pltpu
from jax.sharding import PartitionSpec as P

MESH = pl.DeviceIdType.MESH
GROUP = 4
LANES = 128
ENDS = (2, 5, 8)
CHUNKS = len(ENDS)
PIECES = 16
LOG2E = math.log2(math.e)


def nt(a, b):
    return lax.dot_general(a, b, (((1,), (1,)), ((), ())), preferred_element_type=jnp.float32)


def nn(a, b):
    return jnp.dot(a, b, preferred_element_type=jnp.float32)


def kernel(
    dp_count, tm_count, x_hbm, *refs,
):
    smalls, refs = refs[:9], refs[9:]
    codes_ref, penalty_ref, *refs = refs
    lengths_ref, plan_ref, win_ref, wdown_ref, wup_ref, wout_ref, rate_ref, gain_ref, wbits_ref = refs[:9]
    small_sem, *refs = refs[9:]
    (
        x_ref, wt, narrow, dec, drv, reach, local, reach0, local0, ent, leave, enter, states, mixed, wb,
        onehot, pick, len_b, logits, sums, sendbuf, recvbuf, tmbuf, zbuf, ybuf,
        x_sem, p1_send, p1_recv, p2_send, p2_recv, xs_send, xs_recv, sib_send, sib_recv,
        reach_send, reach_recv, local_send, local_recv, chain_send, chain_recv, fwd_send,
        a2a_send, a2a_recv, sum_send, sum_recv,
    ) = refs
    frames, rows, width = x_ref.shape
    n = math.isqrt(dp_count)
    quarter = width // 4
    piece = rows // PIECES
    ends = [end * rows // 8 for end in ENDS]
    starts = [0] + ends[:-1]
    parts_of = [end - start for start, end in zip(starts, ends)]
    tile = min(256, width)
    tiles = width // tile
    bits = wbits_ref.shape[0]
    packed = bits * frames
    chips = tm_count // 2
    me = lax.axis_index("dp")
    tm = lax.axis_index("tm")
    y, z = me // n, me % n
    chip, core = tm // 2, tm % 2
    odd = chip % 2
    major = y * (1 - core) + z * core
    minor = z * (1 - core) + y * core
    mine = 2 * core + odd
    other = 2 * core + 1 - odd
    sibling = tm + 1 - 2 * core
    next_chip = ((chip + 1) % chips) * 2 + core
    last_chip = ((chip + chips - 1) % chips) * 2 + core

    def dp_of(major_id, minor_id):
        return (major_id * n + minor_id) * (1 - core) + (minor_id * n + major_id) * core

    def on_core(make):
        pl.when(core == 0)(lambda: make(0))
        pl.when(core == 1)(lambda: make(1))

    near = n // 4
    items = [(0, 0, n)]
    if n == 2:
        items += [(1, 0, n)]
    else:
        items += [(o, 0, n) for step in range(1, n // 2) for o in (-step, step)]
        items += [(n // 2, 0, n // 2), (n // 2, n // 2, n // 2)]
    early = 2 * near if n > 2 else 1

    x_copy = pltpu.make_async_copy(x_hbm, x_ref, x_sem)
    barrier = pltpu.get_barrier_semaphore()

    def greet(dp_id, tm_id):
        pl.semaphore_signal(barrier, inc=1, device_id=(dp_id, tm_id), device_id_type=MESH)

    for step in range(1, n):
        greet(dp_of(major, (minor + step) % n), tm)
    for step in range(1, n):
        greet(dp_of((major + step) % n, minor), tm)
    for step in range(1, tm_count):
        greet(me, (tm + step) % tm_count)

    small_copies = [
        pltpu.make_async_copy(source, target, small_sem.at[i])
        for i, (source, target) in enumerate(zip(smalls, (
            lengths_ref, plan_ref, win_ref, wdown_ref, wup_ref, wout_ref, rate_ref, gain_ref, wbits_ref
        )))
    ]
    for i in (2, 5, 3, 4, 6, 0, 1, 7, 8):
        small_copies[i].start()
    x_copy.start()
    small_copies[2].wait()
    small_copies[5].wait()

    wt[0, mine, y, z] = win_ref[:, pl.ds(pl.multiple_of(mine * quarter, quarter), quarter)]
    for i in range(2):
        start = pl.multiple_of((2 * core + i) * quarter, quarter)
        wt[1, 2 * core + i, y, z] = wout_ref[:, pl.ds(start, quarter)]

    @pl.when(chip == 0)
    def _():
        ent[...] = jnp.zeros_like(ent)

    recvbuf[...] = jnp.zeros_like(recvbuf)
    pl.semaphore_wait(barrier, 2 * (n - 1) + (tm_count - 1))

    def remote(ref, send, recv, device):
        return pltpu.make_async_remote_copy(
            src_ref=ref, dst_ref=ref, send_sem=send, recv_sem=recv,
            device_id=device, device_id_type=MESH,
        )

    firsts, counts = (mine, 2 * core), (1, 2)

    def group(w, c, major_id, first=None, low=0, count=n):
        quarters = pl.ds(firsts[w] if first is None else first, counts[w])
        if c == 0:
            return wt.at[w, quarters, major_id, pl.ds(low, count)]
        return wt.at[w, quarters, pl.ds(low, count), major_id]

    def at(offset):
        return (major + n + offset) % n

    def held(w, c, item, first=None):
        offset, low, count = items[item]
        return group(w, c, at(offset), first, low, count)

    def quarters_of(w):
        return pl.ds(firsts[w], counts[w])

    def p1_start(w):
        for step in range(1, n):
            remote(
                wt.at[w, quarters_of(w), y, z], p1_send.at[w], p1_recv.at[w],
                (dp_of(major, (minor + step) % n), tm),
            ).start()

    def p1_all(w):
        some = wt.at[w, quarters_of(w), 0, pl.ds(0, n - 1)]
        return remote(some, p1_send.at[w], p1_recv.at[w], (me, sibling))

    def p2_all(w):
        some = wt.at[w, quarters_of(w), pl.ds(0, n - 1)]
        return remote(some, p2_send.at[w], p2_recv.at[w, 0], (me, sibling))

    def send_group(w, piece_ref, item, toward):
        remote(
            piece_ref, p2_send.at[w], p2_recv.at[w, item - 1], (dp_of(at(toward), minor), tm)
        ).start()

    def near_sends(w):
        p1_all(w).wait_recv()

        def make(c):
            for item in range(1, early + 1):
                send_group(w, group(w, c, major), item, -items[item][0])
            forward(w, c, 0)
        on_core(make)

    def far_sends(w, c, item):
        offset = items[item][0]
        if n == 2 or item > early:
            return
        side = 1 if offset > 0 else -1
        if abs(offset) + near < n // 2:
            send_group(w, held(w, c, item), items.index((offset + side * near, 0, n)), -side * near)
        else:
            low = 0 if side < 0 else n // 2
            target = items.index((n // 2, low, n // 2))
            send_group(w, group(w, c, at(offset), None, low, n // 2), target, -side * near)

    def forward(w, c, item):
        if w == 0:
            target = next_chip if item % 2 == 0 and item < n - 1 else last_chip
            remote(held(w, c, item), xs_send, xs_recv.at[item], (me, target)).start()
        remote(held(w, c, item), sib_send.at[w], sib_recv.at[w], (me, sibling)).start()

    def arrive(w, item):
        def make(c):
            remote(
                held(w, c, item), p2_send.at[w], p2_recv.at[w, item - 1], (me, sibling)
            ).wait_recv()
            far_sends(w, c, item)
            forward(w, c, item)
        on_core(make)

    def x_arrive(item):
        def make(c):
            theirs = held(0, c, item, other)
            remote(theirs, xs_send, xs_recv.at[item], (me, sibling)).wait_recv()
            remote(theirs, sib_send.at[0], sib_recv.at[0], (me, sibling)).start()
        on_core(make)

    def sibling_arrived(w):
        theirs = wt.at[w, pl.ds(2 * (1 - core), 2)]
        remote(theirs, sib_send.at[w], sib_recv.at[w], (me, sibling)).wait_recv()

    def small_things():
        for i in (0, 1, 7, 8):
            small_copies[i].wait()
        first = tm * frames
        lengths = jnp.broadcast_to(lengths_ref[...].astype(jnp.float32), (LANES, rows))
        len_b[...] = lengths.T - first.astype(jnp.float32)
        spread = dp_count * 8
        slot = lax.broadcasted_iota(jnp.int32, (rows, spread), 1)
        source = lax.broadcasted_iota(jnp.int32, (rows, spread), 0)
        kept = slot % 8 < GROUP
        expand = jnp.where(kept & ((slot // 8) * GROUP + slot % 8 == source), 1.0, 0.0)
        expand = expand.astype(jnp.bfloat16)
        pick[...] = expand.T
        plan_rows = jnp.broadcast_to(plan_ref[...].astype(jnp.float32), (8, rows))
        wanted = nn(plan_rows.astype(jnp.bfloat16), expand)[0:1]
        chosen = jnp.where(kept & (wanted == source.astype(jnp.float32)), 1.0, 0.0)
        onehot[...] = chosen.T.astype(jnp.bfloat16)
        place = lax.broadcasted_iota(jnp.int32, (LANES, bits), 0)
        bit = lax.broadcasted_iota(jnp.int32, (LANES, bits), 1)
        chooser = jnp.where(place == bit, 1.0, 0.0).astype(jnp.bfloat16)
        wb[...] = nn(chooser, wbits_ref[...]).astype(jnp.bfloat16)
        sums[...] = jnp.zeros_like(sums)

    def narrowing():
        for i in (3, 4, 6):
            small_copies[i].wait()
        x_copy.wait()
        for t in range(frames):
            narrow[t] = nt(x_ref[t], wdown_ref[...]).astype(jnp.bfloat16)

    def decays(t):
        for i in range(tiles):
            cols = slice(i * tile, (i + 1) * tile)
            u = nn(narrow[t], wup_ref[:, cols]) * LOG2E
            soft = jnp.maximum(u, 0.0) + jnp.log2(1.0 + jnp.exp2(-jnp.abs(u)))
            d = jnp.exp2(-rate_ref[:, cols] * soft)
            dec[t, :, cols] = d
            reach[:, cols] = d if t == 0 else reach[:, cols] * d

    def decay_frames(low, high):
        for t in range(low, min(high, frames)):
            decays(t)

    count = len(items)
    p1_start(0)
    narrowing()
    decay_frames(0, 1)
    near_sends(0)
    p1_start(1)
    decay_frames(1, 3)
    for item in range(1, early + 1):
        arrive(0, item)
    near_sends(1)
    decay_frames(3, 4)
    x_done = 0
    for item in range(early + 1, count):
        x_arrive(x_done)
        x_done += 1
        arrive(0, item)
    decay_frames(4, frames)

    @pl.when(core == 0)
    def _():
        pltpu.make_async_remote_copy(
            src_ref=reach, dst_ref=reach0, send_sem=reach_send, recv_sem=reach_recv,
            device_id=(me, sibling), device_id_type=MESH,
        ).start()

    small_things()
    while x_done < count:
        x_arrive(x_done)
        x_done += 1

    def weight_rows(w, i):
        per = n // tiles
        all_quarters = [wt[w, q, i * per:(i + 1) * per].reshape(tile, quarter) for q in range(4)]
        return jnp.concatenate(all_quarters, axis=1)

    def valid_of(k, t):
        rs = slice(starts[k], ends[k])
        return jnp.where(len_b[rs, :] > float(t), 1.0, 0.0)

    def drives(k):
        rs, part = slice(starts[k], ends[k]), parts_of[k]
        left_side = x_ref[:, rs, :].reshape(frames * part, width)
        for i in range(tiles):
            cols = slice(i * tile, (i + 1) * tile)
            pushed = nt(left_side, weight_rows(0, i)).reshape(frames, part, tile)
            running = None
            for t in range(frames):
                mask = jnp.concatenate([valid_of(k, t)] * max(1, tile // LANES), axis=1)[:, :tile]
                now = pushed[t] * mask
                drv[t, rs, cols] = now
                running = now if t == 0 else dec[t, rs, cols] * running + now
            local[rs, cols] = running

        @pl.when(core == 0)
        def _():
            pltpu.make_async_remote_copy(
                src_ref=local.at[pl.ds(starts[k], part)], dst_ref=local0.at[pl.ds(starts[k], part)],
                send_sem=local_send.at[k], recv_sem=local_recv.at[k],
                device_id=(me, sibling), device_id_type=MESH,
            ).start()

    def local_wait(k):
        rs = pl.ds(starts[k], parts_of[k])
        remote(local0.at[rs], local_send.at[k], local_recv.at[k], (me, sibling)).wait_recv()

    def reach_wait():
        remote(reach0, reach_send, reach_recv, (me, sibling)).wait_recv()

    def pass_on(j, sends=True, receives=True):
        rs = pl.ds(pl.multiple_of(j * piece, piece), piece)
        if receives:
            remote(ent.at[j], chain_send.at[j], chain_recv.at[j], (me, sibling)).wait_recv()
            remote(ent.at[j], fwd_send.at[j], chain_recv.at[j], (me, sibling)).start()
            between = reach0[rs, :] * ent[j].astype(jnp.float32) + local0[rs, :]
        else:
            between = local0[rs, :]
        enter[rs, :] = between
        if sends:
            leave[j] = (reach[rs, :] * between + local[rs, :]).astype(jnp.bfloat16)
            pltpu.make_async_remote_copy(
                src_ref=leave.at[j], dst_ref=ent.at[j],
                send_sem=chain_send.at[j], recv_sem=chain_recv.at[j],
                device_id=(me, next_chip), device_id_type=MESH,
            ).start()

    def pass_chunk(k, sends, receives):
        if k == 0:
            reach_wait()
        local_wait(k)
        for j in range(starts[k] // piece, ends[k] // piece):
            pass_on(j, sends, receives)

    def pass_half(h):
        if h == 0:
            reach_wait()
        for k in range(CHUNKS):
            if (starts[k] >= rows // 2) == (h == 1):
                local_wait(k)

        def step(j, carry):
            pass_on(j)
            return carry

        lax.fori_loop(h * PIECES // 2, (h + 1) * PIECES // 2, step, 0)

    def outputs(k):
        rs, part = slice(starts[k], ends[k]), parts_of[k]
        count = frames * part
        for i in range(tiles):
            cols = slice(i * tile, (i + 1) * tile)
            s = enter[rs, cols]
            for t in range(frames):
                s = dec[t, rs, cols] * s + drv[t, rs, cols]
                states[t, 0:part, cols] = s.astype(jnp.bfloat16)
        left_side = states[:, 0:part].reshape(count, width)
        square = None
        for i in range(tiles):
            cols = slice(i * tile, (i + 1) * tile)
            x = x_ref[:, rs, cols].reshape(count, tile).astype(jnp.float32)
            m = x + nt(left_side, weight_rows(1, i))
            mixed[0:count, cols] = m
            square = m * m if i == 0 else square + m * m
        scaling = lax.rsqrt(jnp.sum(square, axis=1, keepdims=True) * (1.0 / width) + 1e-06)
        normed = (mixed[0:count] * scaling * gain_ref[...]).astype(jnp.bfloat16)
        by_frame = nt(normed, wb[...])
        values = by_frame[0:part]
        for t in range(1, frames):
            values = values + pltpu.roll(by_frame[t * part:(t + 1) * part], t * bits, axis=1)
        logits[rs, :] = values.astype(jnp.bfloat16)
        lane = lax.broadcasted_iota(jnp.int32, (part, LANES), 1)
        frame = (lane // bits).astype(jnp.float32)
        weight = jnp.where((len_b[rs, :] > frame) & (lane < packed), 1.0, 0.0)
        scaled = 4.0 * values
        size = jnp.abs(scaled)
        e = jnp.exp(-size)
        inverse = 1.0 / (1.0 + e)
        chance = jnp.where(scaled >= 0.0, inverse, e * inverse)
        entropy = jnp.log(1.0 + e) + size * e * inverse
        commit = jnp.square(jnp.abs(values) - 1.0)
        for row, value in enumerate((chance, entropy, commit, None)):
            kept = weight if value is None else value * weight
            sums[row:row + 1, :] += jnp.sum(kept, axis=0, keepdims=True)

    is_core1 = core == 1
    sibling_arrived(0)
    for k in range(CHUNKS):
        drives(k)
        if k >= 1:
            @pl.when(is_core1 & (chip == 0))
            def _():
                pass_chunk(k - 1, True, False)
        if k == 0:
            for item in range(1, early + 1):
                arrive(1, item)

    @pl.when(is_core1 & (chip == 0))
    def _():
        pass_chunk(CHUNKS - 1, True, False)

    @pl.when(is_core1 & (chip == 1) & (chip < chips - 1))
    def _():
        pass_half(0)
        pass_half(1)

    @pl.when(is_core1 & (chip > 1) & (chip < chips - 1))
    def _():
        pass_half(0)

    for item in range(early + 1, count):
        arrive(1, item)

    @pl.when(is_core1 & (chip > 1) & (chip < chips - 1))
    def _():
        pass_half(1)

    sibling_arrived(1)
    for k in range(CHUNKS):
        @pl.when(is_core1 & (chip == chips - 1))
        def _():
            pass_chunk(k, False, True)

        @pl.when(core == 0)
        def _():
            for j in range(starts[k] // piece, ends[k] // piece):
                @pl.when(chip > 0)
                def _():
                    remote(ent.at[j], fwd_send.at[j], chain_recv.at[j], (me, sibling)).wait_recv()

                enter[j * piece:(j + 1) * piece, :] = ent[j].astype(jnp.float32)

        outputs(k)

    folded = sums[...]
    folded = folded + pltpu.roll(folded, LANES - 3 * bits, axis=1)
    folded = (
        folded + pltpu.roll(folded, LANES - bits, axis=1)
        + pltpu.roll(folded, LANES - 2 * bits, axis=1)
    )
    is_bit = lax.broadcasted_iota(jnp.int32, (1, LANES), 1) < bits
    one_row = jnp.zeros((1, LANES), jnp.float32)
    for row in range(4):
        kept = jnp.where(is_bit, folded[row:row + 1], 0.0)
        one_row = one_row + (pltpu.roll(kept, row * bits, axis=1) if row else kept)

    def share(buffer, own, stage, value, peer_of):
        buffer[own, 0:1] = value
        for step in range(1, buffer.shape[0]):
            remote(
                buffer.at[own, pl.ds(0, 1)], sum_send.at[stage], sum_recv.at[stage], peer_of(step)
            ).start()

    def shared(buffer, stage):
        return remote(
            buffer.at[pl.ds(0, buffer.shape[0] - 1), pl.ds(0, 1)], sum_send.at[stage], sum_recv.at[stage],
            (me, sibling),
        )

    def total_of(buffer, stage):
        shared(buffer, stage).wait_recv()
        total = buffer[0, 0:1]
        for i in range(1, buffer.shape[0]):
            total = total + buffer[i, 0:1]
        return total

    share(tmbuf, tm, 0, one_row, lambda step: (me, (tm + step) % tm_count))
    dealt = nn(onehot[...], logits[...])
    sendbuf[...] = dealt.reshape(dp_count, 8, LANES)
    recvbuf[me, 0:GROUP] = sendbuf[me, 0:GROUP]

    def from_far(i):
        return n // 2 + (i // 2) * (1 - 2 * (i % 2)) - i % 2

    def deal(step):
        peer = (y + from_far(step // n)) % n * n + (z + from_far(step % n)) % n
        pltpu.make_async_remote_copy(
            src_ref=sendbuf.at[peer, pl.ds(0, GROUP)], dst_ref=recvbuf.at[me, pl.ds(0, GROUP)],
            send_sem=a2a_send, recv_sem=a2a_recv, device_id=(peer, tm), device_id_type=MESH,
        ).start()

    unrolled = 3 if (dp_count - 1) % 3 == 0 else 1

    def deal_some(i, carry):
        for j in range(unrolled):
            deal(i * unrolled + j)
        return carry

    lax.fori_loop(0, (dp_count - 1) // unrolled, deal_some, 0)

    share(zbuf, z, 1, total_of(tmbuf, 0), lambda step: (y * n + (z + step) % n, tm))

    for w in range(2):
        p1_all(w).wait_send()
        p2_all(w).wait_send()
        ours = wt.at[w, pl.ds(2 * core, 2)]
        remote(ours, sib_send.at[w], sib_recv.at[w], (me, sibling)).wait_send()
    remote(wt.at[0, mine], xs_send, xs_recv.at[0], (me, sibling)).wait_send()

    @pl.when(core == 0)
    def _():
        remote(reach, reach_send, reach_recv, (me, sibling)).wait_send()
        for k in range(CHUNKS):
            rs = pl.ds(starts[k], parts_of[k])
            remote(local.at[rs], local_send.at[k], local_recv.at[k], (me, sibling)).wait_send()

    @pl.when(is_core1)
    def _():
        for j in range(PIECES):
            @pl.when(chip < chips - 1)
            def _():
                remote(leave.at[j], chain_send.at[j], chain_recv.at[j], (me, sibling)).wait_send()

            @pl.when(chip > 0)
            def _():
                remote(ent.at[j], fwd_send.at[j], chain_recv.at[j], (me, sibling)).wait_send()

    arrived = remote(
        recvbuf.at[pl.ds(0, dp_count - 1), pl.ds(0, GROUP)], a2a_send, a2a_recv, (me, sibling)
    )
    share(ybuf, y, 2, total_of(zbuf, 1), lambda step: ((y + step) % n * n + z, tm))
    for stage, buffer in enumerate((tmbuf, zbuf)):
        shared(buffer, stage).wait_send()
    arrived.wait_send()
    arrived.wait_recv()
    turned = recvbuf[...].reshape(dp_count * 8, LANES).T.astype(jnp.bfloat16)
    placed = nn(turned, pick[...])
    for t in range(frames):
        codes_ref[t] = placed[t * bits:(t + 1) * bits, :].astype(jnp.bfloat16)

    everything = total_of(ybuf, 2)
    parts = [everything] + [pltpu.roll(everything, LANES - row * bits, axis=1) for row in (1, 2, 3)]
    marginal = jnp.where(is_bit, parts[0] / parts[3], 0.5)
    terms = -marginal * jnp.log(marginal) - (1.0 - marginal) * jnp.log(1.0 - marginal)
    slots = 1.0 / float(rows * dp_count * frames * tm_count)
    shares = (parts[1] + 0.25 * parts[2]) * slots - terms
    penalty_ref[0, 0] = jnp.sum(jnp.where(is_bit, shares, 0.0))
    shared(ybuf, 2).wait_send()


def shards(latents, lengths, plan, w_in, w_down, w_up, w_out, rate, gain, w_bits):
    rows, frames, width = latents.shape
    dp_count, tm_count = lax.axis_size("dp"), lax.axis_size("tm")
    n = math.isqrt(dp_count)
    bits = w_bits.shape[1]
    narrow_width = w_down.shape[1]
    part = rows * 3 // 8
    block = width // dp_count
    bf16, f32 = jnp.bfloat16, jnp.float32
    dma = pltpu.SemaphoreType.DMA
    codes, penalty = pl.pallas_call(
        functools.partial(kernel, dp_count, tm_count),
        out_shape=(
            pltpu.VMEM((frames, bits, rows), bf16),
            jax.ShapeDtypeStruct((1, 1), f32),
        ),
        in_specs=[pl.BlockSpec(memory_space=pl.ANY)] * 10,
        out_specs=(pl.BlockSpec(memory_space=pltpu.VMEM), pl.BlockSpec(memory_space=pltpu.SMEM)),
        scratch_shapes=[
            pltpu.VMEM((1, rows), jnp.int32),
            pltpu.VMEM((1, rows), jnp.int32),
            pltpu.VMEM((block, width), bf16),
            pltpu.VMEM((narrow_width, width), bf16),
            pltpu.VMEM((narrow_width, width), bf16),
            pltpu.VMEM((block, width), bf16),
            pltpu.VMEM((1, width), f32),
            pltpu.VMEM((1, width), f32),
            pltpu.VMEM((bits, width), bf16),
            dma((9,)),
            pltpu.VMEM((frames, rows, width), bf16),
            pltpu.VMEM((2, 4, n, n, block, width // 4), bf16),
            pltpu.VMEM((frames, rows, narrow_width), bf16),
            pltpu.VMEM((frames, rows, width), f32),
            pltpu.VMEM((frames, rows, width), f32),
            pltpu.VMEM((rows, width), f32),
            pltpu.VMEM((rows, width), f32),
            pltpu.VMEM((rows, width), f32),
            pltpu.VMEM((rows, width), f32),
            pltpu.VMEM((PIECES, rows // PIECES, width), bf16),
            pltpu.VMEM((PIECES, rows // PIECES, width), bf16),
            pltpu.VMEM((rows, width), f32),
            pltpu.VMEM((frames, part, width), bf16),
            pltpu.VMEM((frames * part, width), f32),
            pltpu.VMEM((LANES, width), bf16),
            pltpu.VMEM((dp_count * 8, rows), bf16),
            pltpu.VMEM((dp_count * 8, rows), bf16),
            pltpu.VMEM((rows, LANES), f32),
            pltpu.VMEM((rows, LANES), bf16),
            pltpu.VMEM((8, LANES), f32),
            pltpu.VMEM((dp_count, 8, LANES), f32),
            pltpu.VMEM((dp_count, 8, LANES), f32),
            pltpu.VMEM((tm_count, 8, LANES), f32),
            pltpu.VMEM((n, 8, LANES), f32),
            pltpu.VMEM((n, 8, LANES), f32),
            dma,
            dma((2,)), dma((2,)), dma((2,)), dma((2, n)),
            dma, dma((n + 1,)), dma((2,)), dma((2,)),
            dma, dma, dma((CHUNKS,)), dma((CHUNKS,)),
            dma((PIECES,)), dma((PIECES,)), dma((PIECES,)),
            dma, dma, dma((3,)), dma((3,)),
        ],
        compiler_params=pltpu.CompilerParams(
            collective_id=0, has_side_effects=True, vmem_limit_bytes=56 * 1024 * 1024
        ),
    )(
        jnp.transpose(latents, (1, 0, 2)), lengths.reshape(1, rows), plan.reshape(1, rows),
        w_in.T, w_down.T, w_up, w_out.T, rate.reshape(1, width), gain.reshape(1, width), w_bits.T,
    )
    return jnp.transpose(codes, (1, 0, 2)), penalty[0, 0]


def solution(mesh):
    return jax.shard_map(
        shards,
        mesh=mesh,
        in_specs=(
            P("dp", "tm", None),
            P("dp"),
            P("dp"),
            P(None, "dp"),
            P(),
            P(),
            P(None, "dp"),
            P(),
            P(),
            P(),
        ),
        out_specs=(P(None, "tm", "dp"), P()),
        check_vma=False,
    )
```
